128 devices in a mesh: head: 8 (over y_lo, x), blk: 16 (over y_hi, z, core).
Axes of the slice: x: 4, y: 4 (y_hi: 2, y_lo: 2; y = y_hi * 2 + y_lo), z: 4, core: 2. Of those that a mesh axis runs over, the one named last changes fastest.
Arguments:
- queries: bfloat16 [32768, 1024], P(('blk', 'head'))
- key_in: bfloat16 [32768, 1024], P(('blk', 'head'))
- values: bfloat16 [32768, 1024], P(('blk', 'head')), may hold values from -6 to 6
- grad_out: bfloat16 [32768, 1024], P(('blk', 'head')), may hold values from -6 to 6
- block_list: int32 [256, 16], replicated, may hold values from 0 to 255, as said below
Outputs:
- grad_query: bfloat16 [32768, 1024], P(('blk', 'head'))
- grad_key: bfloat16 [32768, 1024], P(('blk', 'head'))
- grad_value: bfloat16 [32768, 1024], P(('blk', 'head'))
The draws below stay inside these ranges and needn't reach their ends.
Inputs may be any that keep to these rules, and one draw needn't show every extreme that they name: `block_list`: the first four entries of row b are b, b - 1, b - 2, b - 3, each raised to 0 where negative; every other entry is a multiple of 16 not above b; entries may repeat.
All inputs are finite; a program needn't handle non-finite values.
Results may differ from the reference program's by a relative error of at most 0.024.
Values may be sent and summed in bfloat16 or wider, within the bound.
A program may use at most 192 MiB of HBM per device.

```python
import math
import jax
import jax.numpy as jnp
from jax import lax

HEADS = 8
DH = 128
QBLK = 128
MAXB = 16
SEQ = 32768
NQB = 256
SEGB = 16


def draw_key_in(key, part):
    key = jax.random.fold_in(key, 11)
    result = jax.random.normal(key, (SEQ, HEADS * DH), jnp.float32)
    return result.astype(jnp.bfloat16)


def draw_queries(key, part):
    key = jax.random.fold_in(key, 12)
    result = jax.random.normal(key, (SEQ, HEADS * DH), jnp.float32)
    return result.astype(jnp.bfloat16)


def draw_block_list(key, part):
    key = jax.random.fold_in(key, 13)
    blocks = jnp.arange(NQB, dtype=jnp.int32)[:, None]
    window = jnp.maximum(blocks - jnp.arange(4, dtype=jnp.int32)[None, :], 0)
    span = blocks // SEGB + 1
    extra = jax.random.randint(key, (NQB, MAXB - 4), 0, 1 << 20, dtype=jnp.int32) % span * SEGB
    return jnp.concatenate([window, extra], axis=1).astype(jnp.int32)


def steps_of(rng, extent, shards, least, high):
    def one(dim, blocks):
        steps = jax.random.uniform(jax.random.fold_in(jax.random.fold_in(rng, 6), dim), (blocks,), jnp.float32, least / len(shards), high / len(shards))
        return jnp.repeat(jnp.exp(steps), extent[dim] // blocks).reshape((-1,) + (1,) * (len(extent) - dim - 1))

    gain = one(*shards[0])
    for cut in shards[1:]:
        gain = gain * one(*cut)
    return gain


def noise(rng, dims, deviation, most, cuts=(), kind=jnp.bfloat16):
    values = jax.random.normal(rng, dims, jnp.float32) * deviation
    if len(cuts) > 0:
        values = steps_of(rng, dims, cuts, -0.22, 0.18) * values
    return jnp.clip(values, min=-most, max=most).astype(kind)


def setup_inputs(seed: int = 0) -> dict:
    splits = jax.random.split(jax.random.key(seed), 6)
    return {
        "queries": draw_queries(jax.random.fold_in(splits[5], 71), 0),
        "key_in": draw_key_in(jax.random.fold_in(splits[5], 71), 0),
        "values": noise(splits[2], (SEQ, HEADS * DH), 1.0, 6.0, ((0, 128),)),
        "grad_out": noise(splits[3], (SEQ, HEADS * DH), 1.0, 6.0, ((0, 128),)),
        "block_list": draw_block_list(jax.random.fold_in(splits[5], 71), 0),
    }


def reference(queries, key_in, values, grad_out, block_list):
    num_blocks = SEQ // QBLK
    score_scale = 1.0 / math.sqrt(DH)
    query_blocks = queries.reshape(num_blocks, QBLK, HEADS, DH)
    key_blocks = key_in.reshape(num_blocks, QBLK, HEADS, DH)
    value_blocks = values.reshape(num_blocks, QBLK, HEADS, DH)
    grad_blocks = grad_out.reshape(num_blocks, QBLK, HEADS, DH)

    def block_step(state_now, block_idx):
        key_grads, value_grads = state_now
        block_ids = block_list[block_idx]
        repeated = block_ids[:, None] == block_ids[None, :]
        first_seen = jnp.logical_not(jnp.any(jnp.tril(repeated, -1), axis=1))
        query_here = query_blocks[block_idx].astype(jnp.float32)
        grad_here = grad_blocks[block_idx].astype(jnp.float32)
        keys_here = key_blocks[block_ids].reshape(MAXB * QBLK, HEADS, DH).astype(jnp.float32)
        values_here = value_blocks[block_ids].reshape(MAXB * QBLK, HEADS, DH).astype(jnp.float32)
        query_pos = block_idx * QBLK + jnp.arange(QBLK, dtype=jnp.int32)
        key_pos = (block_ids[:, None] * QBLK + jnp.arange(QBLK, dtype=jnp.int32)[None, :]).reshape(-1)
        live_mask = jnp.repeat(first_seen, QBLK)[None, :] & (key_pos[None, :] <= query_pos[:, None])
        scores = jnp.einsum('qhd,khd->hqk', query_here, keys_here) * score_scale
        highest = lax.optimization_barrier(jnp.max(jnp.where(live_mask, scores, -1e+30), axis=-1))
        weights = jnp.where(live_mask, jnp.exp(scores - highest[..., None]), 0.0)
        totals = lax.optimization_barrier(jnp.sum(weights, axis=-1))
        log_total = highest + jnp.log(totals)
        output = jnp.einsum('hqk,khd->qhd', weights / totals[..., None], values_here).astype(jnp.bfloat16)
        row_dot = lax.optimization_barrier(jnp.sum(grad_here * output.astype(jnp.float32), axis=-1)).T
        probs = jnp.where(live_mask, jnp.exp(scores - log_total[..., None]), 0.0)
        probs_low = lax.optimization_barrier(probs.astype(jnp.bfloat16)).astype(jnp.float32)
        value_part = jnp.einsum('hqk,qhd->khd', probs_low, grad_here)
        grad_prob = jnp.einsum('qhd,khd->hqk', grad_here, values_here)
        grad_score = lax.optimization_barrier((probs * (grad_prob - row_dot[..., None])).astype(jnp.bfloat16)).astype(jnp.float32)
        query_part = (jnp.einsum('hqk,khd->qhd', grad_score, keys_here) * score_scale).astype(jnp.bfloat16)
        key_part = jnp.einsum('hqk,qhd->khd', grad_score, query_here) * score_scale
        key_grads = key_grads.at[block_ids].add(key_part.reshape(MAXB, QBLK, HEADS, DH))
        value_grads = value_grads.at[block_ids].add(value_part.reshape(MAXB, QBLK, HEADS, DH))
        return ((key_grads, value_grads), query_part)
    zeros = jnp.zeros((num_blocks, QBLK, HEADS, DH), jnp.float32)
    (key_grads, value_grads), query_grads = lax.scan(block_step, (zeros, zeros), jnp.arange(num_blocks, dtype=jnp.int32))
    row_width = HEADS * DH
    return (query_grads.reshape(SEQ, row_width), key_grads.reshape(SEQ, row_width).astype(jnp.bfloat16), value_grads.reshape(SEQ, row_width).astype(jnp.bfloat16))
```

```python
import math

import jax
import jax.numpy as jnp
from jax import lax
from jax.experimental import pallas as pl
from jax.experimental.pallas import tpu as pltpu
from jax.sharding import PartitionSpec as P

DH = 128
QBLK = 128
MAXB = 16
SEGB = 16
HALO = 3 * QBLK
CHUNK = 2 * QBLK
MESH = pl.DeviceIdType.MESH
VMEM = pltpu.VMEM
BF16 = jnp.bfloat16
F32 = jnp.float32
DEAD = -3e38
NT = (((1,), (1,)), ((), ()))


def rows_of(start, size):
    return pl.ds(pl.multiple_of(start, QBLK), size)


def remote(src, dst, send, recv, **where):
    return pltpu.make_async_remote_copy(
        src_ref=src,
        dst_ref=dst,
        send_sem=send,
        recv_sem=recv,
        device_id=where,
        device_id_type=MESH,
    )


def greet(heads, blks):
    head, blk = lax.axis_index("head"), lax.axis_index("blk")
    barrier = pltpu.get_barrier_semaphore()
    for step in range(1, heads):
        pl.semaphore_signal(
            barrier, inc=1, device_id={"head": lax.rem(head + step, heads)}, device_id_type=MESH
        )
    for step in range(1, blks):
        pl.semaphore_signal(
            barrier, inc=1, device_id={"blk": lax.rem(blk + step, blks)}, device_id_type=MESH
        )
    pl.semaphore_wait(barrier, heads + blks - 2)


def gather_kernel(
    heads, blks, q, k, v, g, lq, lk, lv, lg, sk, sv, send_in, recv_in, send_sum, recv_sum, send_halo, recv_halo
):
    head, blk = lax.axis_index("head"), lax.axis_index("blk")
    part = q.shape[0]
    rows = heads * part
    arrays = ((k, lk, HALO), (v, lv, HALO), (q, lq, 0), (g, lg, 0))
    greet(heads, blks)

    def into(which, source, there):
        src, dst, skip = arrays[which]
        return remote(
            src.at[:, rows_of(there * DH, DH)],
            dst.at[rows_of(skip + source * part, part)],
            send_in.at[which, there],
            recv_in.at[which, source],
            head=there,
        )

    for which in range(4):
        for step in range(1, heads):
            into(which, head, lax.rem(head + step, heads)).start()
    for src, dst, skip in arrays:
        dst[rows_of(skip + head * part, part), :] = src[:, rows_of(head * DH, DH)]

    def arrive(which, source):
        @pl.when(head != source)
        def _():
            into(which, source, head).wait_recv()

    pairs = ((lk, sk), (lv, sv))

    def summary(which, owner, there):
        src, dst = pairs[which]
        return remote(
            src.at[pl.ds(HALO, QBLK)],
            dst.at[rows_of(owner * QBLK, QBLK)],
            send_sum.at[which, there],
            recv_sum.at[which, owner],
            blk=there,
        )

    def halo(which, there):
        src, _ = pairs[which]
        return remote(
            src.at[pl.ds(rows, HALO)], src.at[pl.ds(0, HALO)], send_halo.at[which], recv_halo.at[which], blk=there
        )

    for which in range(2):
        arrive(which, 0)
        src, dst = pairs[which]
        for step in range(1, blks):
            @pl.when(blk + step < blks)
            def _():
                summary(which, blk, blk + step).start()

        for owner in range(blks):
            @pl.when(owner > blk)
            def _():
                dst[pl.ds(owner * QBLK, QBLK), :] = jnp.zeros((QBLK, DH), BF16)

        dst[rows_of(blk * QBLK, QBLK), :] = src[pl.ds(HALO, QBLK), :]

        for source in range(1, heads):
            arrive(which, source)

        @pl.when(blk + 1 < blks)
        def _():
            halo(which, blk + 1).start()

        @pl.when(blk == 0)
        def _():
            src[pl.ds(0, HALO), :] = jnp.zeros((HALO, DH), BF16)

    for which in range(2, 4):
        for source in range(heads):
            arrive(which, source)

    for which in range(2):
        for step in range(1, blks):
            @pl.when(blk + step < blks)
            def _():
                summary(which, blk, blk + step).wait_send()

        for owner in range(blks - 1):
            @pl.when(owner < blk)
            def _():
                summary(which, owner, blk).wait_recv()

        @pl.when(blk + 1 < blks)
        def _():
            halo(which, blk + 1).wait_send()

        @pl.when(blk > 0)
        def _():
            halo(which, blk).wait_recv()

    for which in range(4):
        for step in range(1, heads):
            into(which, head, lax.rem(head + step, heads)).wait_send()


def attend_kernel(lists, q, k, v, g, sk, sv, dq, dk, dv, dsk, dsv, kt, skt, live, scores, gprob):
    blk = lax.axis_index("blk")
    rows = q.shape[0]
    keys = sk.shape[0]
    chunks = rows // CHUNK
    wide = HALO + CHUNK
    factor = 1.0 / math.sqrt(DH)
    exp2_factor = factor * math.log2(math.e)
    slabs = [(s, CHUNK) for s in range(0, keys, CHUNK)]

    for start in range(0, k.shape[0], QBLK):
        kt[:, pl.ds(start, QBLK)] = k[pl.ds(start, QBLK), :].T
    for start in range(0, keys, QBLK):
        skt[:, pl.ds(start, QBLK)] = sk[pl.ds(start, QBLK), :].T
    for ref in (dk, dv, dsk, dsv):
        ref[...] = jnp.zeros(ref.shape, ref.dtype)

    mine = lists[pl.ds(pl.multiple_of(blk * SEGB, SEGB), SEGB), :]
    summary = lax.broadcasted_iota(jnp.int32, (SEGB, MAXB), 0) * SEGB
    owner = lax.broadcasted_iota(jnp.int32, (SEGB, QBLK), 0) * SEGB
    for block in range(SEGB):
        hit = jnp.where(mine[block : block + 1, :] == summary, 1.0, 0.0)
        seen = jnp.broadcast_to(jnp.max(hit, axis=1, keepdims=True), (SEGB, QBLK))
        far = owner < blk * SEGB + block - 3
        live[block // 2, :, pl.ds((block % 2) * QBLK, QBLK)] = jnp.where(far, seen, 0.0)

    def chunk_step(c, carry):
        base = pl.multiple_of(c * CHUNK, CHUNK)
        here = pl.ds(base, CHUNK)
        window = pl.ds(base, wide)
        queries, grads = q[here, :], g[here, :]
        top = jnp.full((1, CHUNK), DEAD, F32)
        for start, size in slabs:
            raw = lax.dot_general(sk[pl.ds(start, size), :], queries, NT, preferred_element_type=F32)
            for sub in range(0, size, QBLK):
                alive = live[c, pl.ds((start + sub) // QBLK, 1), :] > 0.5
                masked = jnp.where(alive, raw[sub : sub + QBLK] * exp2_factor, DEAD)
                scores[pl.ds(start + sub, QBLK), :] = masked
                top = jnp.maximum(top, jnp.max(masked, axis=0, keepdims=True))
        key_row = lax.broadcasted_iota(jnp.int32, (wide, CHUNK), 0)
        query_row = lax.broadcasted_iota(jnp.int32, (wide, CHUNK), 1)
        alive = (
            (key_row <= query_row + HALO)
            & ((key_row >= QBLK) | (query_row < QBLK))
            & ((blk > 0) | (key_row + base >= HALO))
        )
        raw = lax.dot_general(k[window, :], queries, NT, preferred_element_type=F32)
        masked = jnp.where(alive, raw * exp2_factor, DEAD)
        scores[pl.ds(keys, wide), :] = masked
        top = jnp.maximum(top, jnp.max(masked, axis=0, keepdims=True))

        total = jnp.zeros((1, CHUNK), F32)
        dotted = jnp.zeros((1, CHUNK), F32)
        for start, size in slabs + [(keys, wide)]:
            there = v[window, :] if start == keys else sv[pl.ds(start, size), :]
            gp = lax.dot_general(there, grads, NT, preferred_element_type=F32)
            weight = jnp.exp2(scores[pl.ds(start, size), :] - top)
            scores[pl.ds(start, size), :] = weight
            gprob[pl.ds(start, size), :] = gp
            total += jnp.sum(weight, axis=0, keepdims=True)
            dotted += jnp.sum(weight * gp, axis=0, keepdims=True)
        inverse = 1.0 / total
        row_dot = dotted * inverse

        dq_t = jnp.zeros((DH, CHUNK), F32)
        for start, size in slabs + [(keys, wide)]:
            prob = scores[pl.ds(start, size), :] * inverse
            ds = (prob * (gprob[pl.ds(start, size), :] - row_dot)).astype(BF16)
            value_part = jnp.dot(prob.astype(BF16), grads, preferred_element_type=F32)
            key_part = jnp.dot(ds, queries, preferred_element_type=F32)
            if start == keys:
                dv[window, :] += value_part
                dk[window, :] += key_part
                turned = kt[:, window]
            else:
                dsv[pl.ds(start, size), :] += value_part
                dsk[pl.ds(start, size), :] += key_part
                turned = skt[:, pl.ds(start, size)]
            dq_t += jnp.dot(turned, ds, preferred_element_type=F32)
        dq[here, :] = (dq_t.T * factor).astype(BF16)
        return carry

    lax.fori_loop(0, chunks, chunk_step, 0)


def scatter_kernel(
    heads, blks, dq, dk, dv, dsk, dsv, oq, ok, ov,
    bk, bv, gk, gv, hk, hv, total, send_out, recv_out, send_sum, recv_sum, send_halo, recv_halo,
):
    head, blk = lax.axis_index("head"), lax.axis_index("blk")
    part = oq.shape[0]
    rows = heads * part
    factor = 1.0 / math.sqrt(DH)
    sets = ((dk, dsk, bk, gk, hk, ok, factor), (dv, dsv, bv, gv, hv, ov, 1.0))
    for own, own_sum, out, sums, _, _, scale in sets:
        sums[0] = (own_sum[...] * scale).astype(BF16)
        out[pl.ds(0, HALO), :] = (own[pl.ds(0, HALO), :] * scale).astype(BF16)
    greet(heads, blks)

    def summary(which, owner, source):
        sums = sets[which][3]
        return remote(
            sums.at[0, rows_of(owner * QBLK, QBLK)],
            sums.at[1, rows_of(source * QBLK, QBLK)],
            send_sum.at[which, owner],
            recv_sum.at[which, source],
            blk=owner,
        )

    def halo(which, there):
        _, _, out, _, into, _, _ = sets[which]
        return remote(out.at[pl.ds(0, HALO)], into, send_halo.at[which], recv_halo.at[which], blk=there)

    outs = ((dq, oq, 0), (bk, ok, HALO), (bv, ov, HALO))

    def back(which, source, there):
        src, dst, skip = outs[which]
        return remote(
            src.at[rows_of(skip + there * part, part)],
            dst.at[:, rows_of(source * DH, DH)],
            send_out.at[which, there],
            recv_out.at[which, source],
            head=there,
        )

    def send(which, there):
        src, dst, skip = outs[which]

        @pl.when(head != there)
        def _():
            back(which, head, there).start()

        @pl.when(head == there)
        def _():
            dst[:, rows_of(there * DH, DH)] = src[pl.ds(skip + there * part, part), :]

    for which in range(2):
        for owner in range(blks - 1):
            @pl.when(owner < blk)
            def _():
                summary(which, owner, blk).start()

        @pl.when(blk > 0)
        def _():
            halo(which, blk - 1).start()

    for there in range(heads):
        send(0, there)
    late = [(heads * part - HALO) // part, heads - 1]
    for which in range(2):
        own, _, out, _, _, _, scale = sets[which]
        for there in range(1, late[0]):
            at = pl.ds(HALO + there * part, part)
            out[at, :] = (own[at, :] * scale).astype(BF16)
            send(1 + which, there)
    for which in range(2):
        own, _, out, _, into, _, scale = sets[which]

        @pl.when(blk + 1 < blks)
        def _():
            halo(which, blk).wait_recv()

        first = HALO + late[0] * part
        spare = (heads - late[0]) * part - HALO
        if spare > 0:
            at = pl.ds(first, spare)
            out[at, :] = (own[at, :] * scale).astype(BF16)
        at = pl.ds(rows, HALO)

        @pl.when(blk + 1 < blks)
        def _():
            out[at, :] = (own[at, :] * scale + into[...].astype(F32)).astype(BF16)

        @pl.when(blk + 1 == blks)
        def _():
            out[at, :] = (own[at, :] * scale).astype(BF16)

        for there in range(late[0], heads):
            send(1 + which, there)
    for which in range(2):
        own, own_sum, out, sums, _, _, scale = sets[which]
        total[...] = own[pl.ds(HALO, QBLK), :] + own_sum[rows_of(blk * QBLK, QBLK), :]
        total[...] *= scale
        for source in range(1, blks):
            @pl.when(source > blk)
            def _():
                summary(which, blk, source).wait_recv()
                total[...] += sums[1, pl.ds(source * QBLK, QBLK), :].astype(F32)

        out[pl.ds(HALO, QBLK), :] = total[...].astype(BF16)
        at = pl.ds(HALO + QBLK, part - QBLK)
        out[at, :] = (own[at, :] * scale).astype(BF16)
        send(1 + which, 0)

    for which in range(2):
        for owner in range(blks - 1):
            @pl.when(owner < blk)
            def _():
                summary(which, owner, blk).wait_send()

        @pl.when(blk > 0)
        def _():
            halo(which, blk - 1).wait_send()

    for which in range(3):
        for step in range(1, heads):
            other = lax.rem(head + step, heads)
            back(which, head, other).wait_send()
            back(which, other, head).wait_recv()


def body_of(heads, blks):
    def body(queries, key_in, values, grad_out, block_list):
        part, width = queries.shape
        rows, keys = heads * part, blks * QBLK
        dma = pltpu.SemaphoreType.DMA
        whole = pl.BlockSpec(memory_space=VMEM)

        def shape(*dims, dtype=BF16):
            return jax.ShapeDtypeStruct(dims, dtype)

        comm = dict(has_side_effects=True, vmem_limit_bytes=48 * 1024 * 1024)
        lq, lk, lv, lg, sk, sv = pl.pallas_call(
            lambda *refs: gather_kernel(heads, blks, *refs),
            out_shape=(
                shape(rows, DH),
                shape(HALO + rows, DH),
                shape(HALO + rows, DH),
                shape(rows, DH),
                shape(keys, DH),
                shape(keys, DH),
            ),
            in_specs=[whole] * 4,
            out_specs=[whole] * 6,
            scratch_shapes=[
                dma((4, heads)),
                dma((4, heads)),
                dma((2, blks)),
                dma((2, blks)),
                dma((2,)),
                dma((2,)),
            ],
            compiler_params=pltpu.CompilerParams(collective_id=0, **comm),
            name="gather",
        )(queries, key_in, values, grad_out)
        wide = HALO + CHUNK
        dq, dk, dv, dsk, dsv = pl.pallas_call(
            attend_kernel,
            out_shape=(
                shape(rows, DH),
                shape(HALO + rows, DH, dtype=F32),
                shape(HALO + rows, DH, dtype=F32),
                shape(keys, DH, dtype=F32),
                shape(keys, DH, dtype=F32),
            ),
            in_specs=[whole] * 7,
            out_specs=[whole] * 5,
            scratch_shapes=[
                VMEM((DH, HALO + rows), BF16),
                VMEM((DH, keys), BF16),
                VMEM((rows // CHUNK, SEGB, CHUNK), F32),
                VMEM((keys + wide, CHUNK), F32),
                VMEM((keys + wide, CHUNK), F32),
            ],
            compiler_params=pltpu.CompilerParams(vmem_limit_bytes=48 * 1024 * 1024),
            name="attend",
        )(block_list, lq, lk, lv, lg, sk, sv)
        return pl.pallas_call(
            lambda *refs: scatter_kernel(heads, blks, *refs),
            out_shape=(shape(part, width),) * 3,
            in_specs=[whole] * 5,
            out_specs=[whole] * 3,
            scratch_shapes=[
                VMEM((HALO + rows, DH), BF16),
                VMEM((HALO + rows, DH), BF16),
                VMEM((2, keys, DH), BF16),
                VMEM((2, keys, DH), BF16),
                VMEM((HALO, DH), BF16),
                VMEM((HALO, DH), BF16),
                VMEM((QBLK, DH), F32),
                dma((3, heads)),
                dma((3, heads)),
                dma((2, blks)),
                dma((2, blks)),
                dma((2,)),
                dma((2,)),
            ],
            compiler_params=pltpu.CompilerParams(collective_id=1, **comm),
            name="scatter",
        )(dq, dk, dv, dsk, dsv)

    return body


def solution(mesh):
    placed = P(("blk", "head"), None)
    return jax.shard_map(
        body_of(mesh.shape["head"], mesh.shape["blk"]),
        mesh=mesh,
        in_specs=(placed,) * 4 + (P(),),
        out_specs=(placed,) * 3,
        check_vma=False,
    )
```

```python
import math

import jax
import jax.numpy as jnp
from jax import lax
from jax.experimental import pallas as pl
from jax.experimental.pallas import tpu as pltpu
from jax.sharding import PartitionSpec as P

DH = 128
QBLK = 128
MAXB = 16
SEGB = 16
HALO = 3 * QBLK
CHUNK = 2 * QBLK
WIDE = HALO + CHUNK
MESH = pl.DeviceIdType.MESH
VMEM = pltpu.VMEM
BF16 = jnp.bfloat16
F32 = jnp.float32
DEAD = -3e38
FACTOR = 1.0 / math.sqrt(DH)
NT = (((1,), (1,)), ((), ()))


def aligned(start, size):
    return pl.ds(pl.multiple_of(start, QBLK), size)


def remote(src, dst, send, recv, **where):
    return pltpu.make_async_remote_copy(
        src_ref=src,
        dst_ref=dst,
        send_sem=send,
        recv_sem=recv,
        device_id=where,
        device_id_type=MESH,
    )


def greet(heads, blks):
    head, blk = lax.axis_index("head"), lax.axis_index("blk")
    barrier = pltpu.get_barrier_semaphore()
    for step in range(1, heads):
        pl.semaphore_signal(
            barrier, inc=1, device_id={"head": lax.rem(head + step, heads)}, device_id_type=MESH
        )
    for step in range(1, blks):
        pl.semaphore_signal(
            barrier, inc=1, device_id={"blk": lax.rem(blk + step, blks)}, device_id_type=MESH
        )
    pl.semaphore_wait(barrier, heads + blks - 2)


def mark_live(lists, live):
    blk = lax.axis_index("blk")
    mine = lists[pl.ds(pl.multiple_of(blk * SEGB, SEGB), SEGB), :]
    summary = lax.broadcasted_iota(jnp.int32, (SEGB, MAXB), 0) * SEGB
    owner = lax.broadcasted_iota(jnp.int32, (SEGB, QBLK), 0) * SEGB
    for block in range(SEGB):
        hit = jnp.where(mine[block : block + 1, :] == summary, 1.0, 0.0)
        seen = jnp.broadcast_to(jnp.max(hit, axis=1, keepdims=True), (SEGB, QBLK))
        far = owner < blk * SEGB + block - 3
        live[block // 2, :, pl.ds((block % 2) * QBLK, QBLK)] = jnp.where(far, seen, 0.0)


def attend(c, q, k, v, g, sk, sv, dq, dk, dv, dsk, dsv, kt, skt, live, scores, gprob):
    blk = lax.axis_index("blk")
    keys = sk.shape[0]
    exp2_factor = FACTOR * math.log2(math.e)
    slabs = [(s, CHUNK) for s in range(0, keys, CHUNK)]
    base = pl.multiple_of(c * CHUNK, CHUNK)
    here = pl.ds(base, CHUNK)
    window = pl.ds(base, WIDE)
    queries, grads = q[here, :], g[here, :]
    top = jnp.full((1, CHUNK), DEAD, F32)
    for start, size in slabs:
        raw = lax.dot_general(sk[pl.ds(start, size), :], queries, NT, preferred_element_type=F32)
        for sub in range(0, size, QBLK):
            alive = live[c, pl.ds((start + sub) // QBLK, 1), :] > 0.5
            masked = jnp.where(alive, raw[sub : sub + QBLK] * exp2_factor, DEAD)
            scores[pl.ds(start + sub, QBLK), :] = masked
            top = jnp.maximum(top, jnp.max(masked, axis=0, keepdims=True))
    key_row = lax.broadcasted_iota(jnp.int32, (WIDE, CHUNK), 0)
    query_row = lax.broadcasted_iota(jnp.int32, (WIDE, CHUNK), 1)
    alive = (
        (key_row <= query_row + HALO)
        & ((key_row >= QBLK) | (query_row < QBLK))
        & ((blk > 0) | (key_row + base >= HALO))
    )
    raw = lax.dot_general(k[window, :], queries, NT, preferred_element_type=F32)
    masked = jnp.where(alive, raw * exp2_factor, DEAD)
    scores[pl.ds(keys, WIDE), :] = masked
    top = jnp.maximum(top, jnp.max(masked, axis=0, keepdims=True))

    total = jnp.zeros((1, CHUNK), F32)
    dotted = jnp.zeros((1, CHUNK), F32)
    for start, size in slabs + [(keys, WIDE)]:
        there = v[window, :] if start == keys else sv[pl.ds(start, size), :]
        gp = lax.dot_general(there, grads, NT, preferred_element_type=F32)
        weight = jnp.exp2(scores[pl.ds(start, size), :] - top)
        scores[pl.ds(start, size), :] = weight
        gprob[pl.ds(start, size), :] = gp
        total += jnp.sum(weight, axis=0, keepdims=True)
        dotted += jnp.sum(weight * gp, axis=0, keepdims=True)
    inverse = 1.0 / total
    row_dot = dotted * inverse

    dq_t = jnp.zeros((DH, CHUNK), F32)
    for start, size in slabs + [(keys, WIDE)]:
        prob = scores[pl.ds(start, size), :] * inverse
        ds = (prob * (gprob[pl.ds(start, size), :] - row_dot)).astype(BF16)
        value_part = jnp.dot(prob.astype(BF16), grads, preferred_element_type=F32)
        key_part = jnp.dot(ds, queries, preferred_element_type=F32)
        if start == keys:
            dv[window, :] += value_part
            dk[window, :] += key_part
            turned = kt[:, window]
        else:
            dsv[pl.ds(start, size), :] += value_part
            dsk[pl.ds(start, size), :] += key_part
            turned = skt[:, pl.ds(start, size)]
        dq_t += jnp.dot(turned, ds, preferred_element_type=F32)
    dq[here, :] = (dq_t.T * FACTOR).astype(BF16)


def fused(
    heads, blks, lists, q, k, v, g, oq, ok, ov,
    lq, lk, lv, lg, sk, sv, dq, dk, dv, dsk, dsv, bk, bv, gk, gv, hk, hv, block_sum, kt, skt, live, scores, gprob,
    send_in, recv_in, send_first, recv_first, send_own, send_sum, recv_sum, send_halo, recv_halo,
    send_out, recv_out, keep_out, send_part, recv_part, send_edge, recv_edge,
):
    head, blk = lax.axis_index("head"), lax.axis_index("blk")
    part = q.shape[0]
    rows = heads * part
    keys = blks * QBLK
    rest = part - QBLK

    arrays = ((k, lk, HALO), (v, lv, HALO), (q, lq, 0), (g, lg, 0))

    def into(which, source, there):
        src, dst, skip = arrays[which]
        return remote(
            src.at[:, aligned(there * DH, DH)],
            dst.at[aligned(skip + source * part, part)],
            send_in.at[which, there],
            recv_in.at[which, source],
            head=there,
        )

    def first(which, there):
        src, dst, _ = arrays[which]
        return remote(
            src.at[pl.ds(0, QBLK), aligned(there * DH, DH)],
            dst.at[pl.ds(HALO, QBLK)],
            send_first.at[which, there],
            recv_first.at[which],
            head=there,
        )

    def second(which, there):
        src, dst, _ = arrays[which]
        return remote(
            src.at[pl.ds(QBLK, rest), aligned(there * DH, DH)],
            dst.at[pl.ds(HALO + QBLK, rest)],
            send_in.at[which, there],
            recv_in.at[which, 0],
            head=there,
        )

    def own(which):
        src, dst, skip = arrays[which]
        return pltpu.make_async_copy(
            src.at[:, aligned(head * DH, DH)], dst.at[aligned(skip + head * part, part)], send_own.at[which]
        )

    def other(step):
        return lax.rem(head + step, heads)

    greet(heads, blks)

    @pl.when(head == 0)
    def _():
        for step in range(1, heads):
            for which in range(2):
                first(which, step).start()
        for step in range(1, heads):
            for which in range(2):
                second(which, step).start()

    for which in range(4):
        own(which).start()

    @pl.when(head > 0)
    def _():
        for step in range(1, heads):
            for which in range(2):
                into(which, head, other(step)).start()

    for step in range(1, heads):
        for which in range(2, 4):
            into(which, head, other(step)).start()

    def arrive(which, source):
        @pl.when(head != source)
        def _():
            if which < 2 and isinstance(source, int) and source == 0:
                second(which, head).wait_recv()
            else:
                into(which, source, head).wait_recv()

    pairs = ((lk, sk), (lv, sv))

    def summary(which, owner, there):
        src, dst = pairs[which]
        return remote(
            src.at[pl.ds(HALO, QBLK)],
            dst.at[aligned(owner * QBLK, QBLK)],
            send_sum.at[which, there],
            recv_sum.at[which, owner],
            blk=there,
        )

    def halo(which, there):
        src, _ = pairs[which]
        return remote(
            src.at[pl.ds(rows, HALO)], src.at[pl.ds(0, HALO)], send_halo.at[which], recv_halo.at[which], blk=there
        )

    mark_live(lists, live)
    for ref in (dk, dv, dsk, dsv):
        ref[...] = jnp.zeros(ref.shape, ref.dtype)
    for which in range(4):
        own(which).wait()

    for which in range(2):
        @pl.when(head > 0)
        def _():
            first(which, head).wait_recv()

    for step in range(1, blks):
        @pl.when(blk + step < blks)
        def _():
            for which in range(2):
                summary(which, blk, blk + step).start()

    for which in range(2):
        src, dst = pairs[which]
        for owner in range(blks):
            @pl.when(owner > blk)
            def _():
                dst[pl.ds(owner * QBLK, QBLK), :] = jnp.zeros((QBLK, DH), BF16)

        dst[aligned(blk * QBLK, QBLK), :] = src[pl.ds(HALO, QBLK), :]

    for source in range(heads - 1, -1, -1):
        for which in range(2):
            arrive(which, source)
        if source == heads - 2:
            @pl.when(blk + 1 < blks)
            def _():
                for which in range(2):
                    halo(which, blk + 1).start()

    @pl.when(blk == 0)
    def _():
        for src, _ in pairs:
            src[pl.ds(0, HALO), :] = jnp.zeros((HALO, DH), BF16)

    @pl.when(blk > 0)
    def _():
        for which in range(2):
            halo(which, blk).wait_recv()

    for which in range(2):
        for owner in range(blks - 1):
            @pl.when(owner < blk)
            def _():
                summary(which, owner, blk).wait_recv()

    for start in range(0, HALO + rows, QBLK):
        kt[:, pl.ds(start, QBLK)] = lk[pl.ds(start, QBLK), :].T
    for start in range(0, keys, QBLK):
        skt[:, pl.ds(start, QBLK)] = sk[pl.ds(start, QBLK), :].T

    outs = ((dq, oq, 0), (bk, ok, HALO), (bv, ov, HALO))
    sets = ((dk, dsk, bk, gk, hk, FACTOR), (dv, dsv, bv, gv, hv, 1.0))

    def back(which, source, there):
        src, dst, skip = outs[which]
        return remote(
            src.at[aligned(skip + there * part, part)],
            dst.at[:, aligned(source * DH, DH)],
            send_out.at[which, there],
            recv_out.at[which, source],
            head=there,
        )

    def keep(which):
        src, dst, skip = outs[which]
        return pltpu.make_async_copy(
            src.at[aligned(skip + head * part, part)], dst.at[:, aligned(head * DH, DH)], keep_out.at[which]
        )

    def send(which, there):
        @pl.when(head != there)
        def _():
            back(which, head, there).start()

        @pl.when(head == there)
        def _():
            keep(which).start()

    def partial(which, owner, source):
        sums = sets[which][3]
        return remote(
            sums.at[0, aligned(owner * QBLK, QBLK)],
            sums.at[1, aligned(source * QBLK, QBLK)],
            send_part.at[which, owner],
            recv_part.at[which, source],
            blk=owner,
        )

    def edge(which, there):
        _, _, out, _, from_next, _ = sets[which]
        return remote(out.at[pl.ds(0, HALO)], from_next, send_edge.at[which], recv_edge.at[which], blk=there)

    def finish(which, there):
        acc, _, out, _, _, scale = sets[which]
        at = aligned(HALO + there * part, part)
        out[at, :] = (acc[at, :] * scale).astype(BF16)
        send(1 + which, there)

    def outer(c):
        return (c == 0) | (c >= heads - 2)

    def step_of(step, carry):
        c = lax.rem(head - step + heads, heads)

        @pl.when(step > 0)
        def _():
            for which in range(2, 4):
                into(which, c, head).wait_recv()

        attend(c, lq, lk, lv, lg, sk, sv, dq, dk, dv, dsk, dsv, kt, skt, live, scores, gprob)
        send(0, c)

        @pl.when((step >= 2) & jnp.logical_not(outer(c)))
        def _():
            for which in range(2):
                finish(which, c)

        return carry

    lax.fori_loop(0, heads, step_of, 0)

    for which in range(2):
        acc, acc_sum, out, sums, _, scale = sets[which]
        sums[0] = (acc_sum[...] * scale).astype(BF16)
        for owner in range(blks - 1):
            @pl.when(owner < blk)
            def _():
                partial(which, owner, blk).start()

        out[pl.ds(0, HALO), :] = (acc[pl.ds(0, HALO), :] * scale).astype(BF16)

        @pl.when(blk > 0)
        def _():
            edge(which, blk - 1).start()

    for step in range(2):
        c = lax.rem(head - step + heads, heads)

        @pl.when(jnp.logical_not(outer(c)))
        def _():
            for which in range(2):
                finish(which, c)

    for which in range(2):
        acc, _, out, _, from_next, scale = sets[which]
        spare = 2 * part - HALO
        at = pl.ds(HALO + rows - 2 * part, spare)
        out[at, :] = (acc[at, :] * scale).astype(BF16)
        at = pl.ds(rows, HALO)

        @pl.when(blk + 1 < blks)
        def _():
            edge(which, blk).wait_recv()
            out[at, :] = (acc[at, :] * scale + from_next[...].astype(F32)).astype(BF16)

        @pl.when(blk + 1 == blks)
        def _():
            out[at, :] = (acc[at, :] * scale).astype(BF16)

        for there in range(heads - 2, heads):
            send(1 + which, there)

    for which in range(2):
        acc, acc_sum, out, sums, _, scale = sets[which]
        block_sum[...] = (acc[pl.ds(HALO, QBLK), :] + acc_sum[aligned(blk * QBLK, QBLK), :]) * scale
        for source in range(1, blks):
            @pl.when(source > blk)
            def _():
                partial(which, blk, source).wait_recv()
                block_sum[...] += sums[1, pl.ds(source * QBLK, QBLK), :].astype(F32)

        out[pl.ds(HALO, QBLK), :] = block_sum[...].astype(BF16)
        at = pl.ds(HALO + QBLK, rest)
        out[at, :] = (acc[at, :] * scale).astype(BF16)
        send(1 + which, 0)

    @pl.when(head == 0)
    def _():
        for step in range(1, heads):
            for which in range(2):
                first(which, step).wait_send()
                second(which, step).wait_send()

    @pl.when(head > 0)
    def _():
        for step in range(1, heads):
            for which in range(2):
                into(which, head, other(step)).wait_send()

    for step in range(1, heads):
        for which in range(2, 4):
            into(which, head, other(step)).wait_send()

    for which in range(2):
        for step in range(1, blks):
            @pl.when(blk + step < blks)
            def _():
                summary(which, blk, blk + step).wait_send()

        for owner in range(blks - 1):
            @pl.when(owner < blk)
            def _():
                partial(which, owner, blk).wait_send()

        @pl.when(blk + 1 < blks)
        def _():
            halo(which, blk + 1).wait_send()

        @pl.when(blk > 0)
        def _():
            edge(which, blk - 1).wait_send()

    for which in range(3):
        keep(which).wait()
        for step in range(1, heads):
            back(which, head, other(step)).wait_send()
            back(which, other(step), head).wait_recv()


def body_of(heads, blks):
    def body(queries, key_in, values, grad_out, block_list):
        part, width = queries.shape
        rows, keys = heads * part, blks * QBLK
        dma = pltpu.SemaphoreType.DMA
        whole = pl.BlockSpec(memory_space=VMEM)
        far = pl.BlockSpec(memory_space=pltpu.HBM)
        return pl.pallas_call(
            lambda *refs: fused(heads, blks, *refs),
            out_shape=(jax.ShapeDtypeStruct((part, width), BF16),) * 3,
            in_specs=[whole] + [far] * 4,
            out_specs=[far] * 3,
            scratch_shapes=[
                VMEM((rows, DH), BF16),
                VMEM((HALO + rows, DH), BF16),
                VMEM((HALO + rows, DH), BF16),
                VMEM((rows, DH), BF16),
                VMEM((keys, DH), BF16),
                VMEM((keys, DH), BF16),
                VMEM((rows, DH), BF16),
                VMEM((HALO + rows, DH), F32),
                VMEM((HALO + rows, DH), F32),
                VMEM((keys, DH), F32),
                VMEM((keys, DH), F32),
                VMEM((HALO + rows, DH), BF16),
                VMEM((HALO + rows, DH), BF16),
                VMEM((2, keys, DH), BF16),
                VMEM((2, keys, DH), BF16),
                VMEM((HALO, DH), BF16),
                VMEM((HALO, DH), BF16),
                VMEM((QBLK, DH), F32),
                VMEM((DH, HALO + rows), BF16),
                VMEM((DH, keys), BF16),
                VMEM((rows // CHUNK, SEGB, CHUNK), F32),
                VMEM((keys + WIDE, CHUNK), F32),
                VMEM((keys + WIDE, CHUNK), F32),
                dma((4, heads)),
                dma((4, heads)),
                dma((2, heads)),
                dma((2,)),
                dma((4,)),
                dma((2, blks)),
                dma((2, blks)),
                dma((2,)),
                dma((2,)),
                dma((3, heads)),
                dma((3, heads)),
                dma((3,)),
                dma((2, blks)),
                dma((2, blks)),
                dma((2,)),
                dma((2,)),
            ],
            compiler_params=pltpu.CompilerParams(
                collective_id=0, has_side_effects=True, vmem_limit_bytes=62 * 1024 * 1024
            ),
            name="attention_backward",
        )(block_list, queries, key_in, values, grad_out)

    return body


def solution(mesh):
    placed = P(("blk", "head"), None)
    return jax.shard_map(
        body_of(mesh.shape["head"], mesh.shape["blk"]),
        mesh=mesh,
        in_specs=(placed,) * 4 + (P(),),
        out_specs=(placed,) * 3,
        check_vma=False,
    )
```

```python
import math

import jax
import jax.numpy as jnp
from jax import lax
from jax.experimental import pallas as pl
from jax.experimental.pallas import tpu as pltpu
from jax.sharding import PartitionSpec as P

DH = 128
QBLK = 128
MAXB = 16
SEGB = 16
HALO = 3 * QBLK
CHUNK = 2 * QBLK
WIDE = HALO + CHUNK
MESH = pl.DeviceIdType.MESH
VMEM = pltpu.VMEM
BF16 = jnp.bfloat16
F32 = jnp.float32
DEAD = -3e38
FACTOR = 1.0 / math.sqrt(DH)
NT = (((1,), (1,)), ((), ()))


def aligned(start, size):
    return pl.ds(pl.multiple_of(start, QBLK), size)


def remote(src, dst, send, recv, **where):
    return pltpu.make_async_remote_copy(
        src_ref=src,
        dst_ref=dst,
        send_sem=send,
        recv_sem=recv,
        device_id=where,
        device_id_type=MESH,
    )


def greet(heads, blks):
    head, blk = lax.axis_index("head"), lax.axis_index("blk")
    barrier = pltpu.get_barrier_semaphore()
    for step in range(1, heads):
        pl.semaphore_signal(
            barrier, inc=1, device_id={"head": lax.rem(head + step, heads)}, device_id_type=MESH
        )
    for step in range(1, blks):
        pl.semaphore_signal(
            barrier, inc=1, device_id={"blk": lax.rem(blk + step, blks)}, device_id_type=MESH
        )
    pl.semaphore_wait(barrier, heads + blks - 2)


def mark_live(lists, live):
    blk = lax.axis_index("blk")
    blocks = lists.shape[1]
    owner = lax.broadcasted_iota(jnp.int32, (SEGB, blocks), 0)
    seen = jnp.zeros((SEGB, blocks), F32)
    for entry in range(MAXB):
        seen = jnp.where(lists[entry : entry + 1, :] == owner * SEGB, 1.0, seen)
    column = lax.broadcasted_iota(jnp.int32, (blocks, CHUNK), 0)
    query = lax.broadcasted_iota(jnp.int32, (blocks, CHUNK), 1) // QBLK
    slot = lax.broadcasted_iota(jnp.int32, (SEGB, CHUNK), 0) * SEGB
    reader = lax.broadcasted_iota(jnp.int32, (SEGB, CHUNK), 1) // QBLK
    for c in range(live.shape[0]):
        first = blk * SEGB + 2 * c
        spread = jnp.where(column == query + first, 1.0, 0.0).astype(BF16)
        chosen = jnp.dot(seen.astype(BF16), spread, preferred_element_type=F32)
        live[c] = jnp.where(slot < reader + (first - 3), chosen, 0.0)


def attend(c, q, k, v, g, sk, sv, dq, dk, dv, dsk, dsv, kt, skt, live, scores, gprob):
    blk = lax.axis_index("blk")
    keys = sk.shape[0]
    exp2_factor = FACTOR * math.log2(math.e)
    slabs = [(s, CHUNK) for s in range(0, keys, CHUNK)]
    base = pl.multiple_of(c * CHUNK, CHUNK)
    here = pl.ds(base, CHUNK)
    window = pl.ds(base, WIDE)
    queries, grads = q[here, :], g[here, :]
    top = jnp.full((1, CHUNK), DEAD, F32)
    for start, size in slabs:
        raw = lax.dot_general(sk[pl.ds(start, size), :], queries, NT, preferred_element_type=F32)
        for sub in range(0, size, QBLK):
            alive = live[c, pl.ds((start + sub) // QBLK, 1), :] > 0.5
            masked = jnp.where(alive, raw[sub : sub + QBLK] * exp2_factor, DEAD)
            scores[pl.ds(start + sub, QBLK), :] = masked
            top = jnp.maximum(top, jnp.max(masked, axis=0, keepdims=True))
    key_row = lax.broadcasted_iota(jnp.int32, (WIDE, CHUNK), 0)
    query_row = lax.broadcasted_iota(jnp.int32, (WIDE, CHUNK), 1)
    alive = (
        (key_row <= query_row + HALO)
        & ((key_row >= QBLK) | (query_row < QBLK))
        & ((blk > 0) | (key_row + base >= HALO))
    )
    raw = lax.dot_general(k[window, :], queries, NT, preferred_element_type=F32)
    masked = jnp.where(alive, raw * exp2_factor, DEAD)
    scores[pl.ds(keys, WIDE), :] = masked
    top = jnp.maximum(top, jnp.max(masked, axis=0, keepdims=True))

    total = jnp.zeros((1, CHUNK), F32)
    dotted = jnp.zeros((1, CHUNK), F32)
    for start, size in slabs + [(keys, WIDE)]:
        there = v[window, :] if start == keys else sv[pl.ds(start, size), :]
        gp = lax.dot_general(there, grads, NT, preferred_element_type=F32)
        weight = jnp.exp2(scores[pl.ds(start, size), :] - top)
        scores[pl.ds(start, size), :] = weight
        gprob[pl.ds(start, size), :] = gp
        total += jnp.sum(weight, axis=0, keepdims=True)
        dotted += jnp.sum(weight * gp, axis=0, keepdims=True)
    inverse = 1.0 / total
    row_dot = dotted * inverse

    dq_t = jnp.zeros((DH, CHUNK), F32)
    for start, size in slabs + [(keys, WIDE)]:
        prob = scores[pl.ds(start, size), :] * inverse
        ds = (prob * (gprob[pl.ds(start, size), :] - row_dot)).astype(BF16)
        value_part = jnp.dot(prob.astype(BF16), grads, preferred_element_type=F32)
        key_part = jnp.dot(ds, queries, preferred_element_type=F32)
        if start == keys:
            dv[window, :] += value_part
            dk[window, :] += key_part
            turned = kt[:, window]
        else:
            dsv[pl.ds(start, size), :] += value_part
            dsk[pl.ds(start, size), :] += key_part
            turned = skt[:, pl.ds(start, size)]
        dq_t += jnp.dot(turned, ds, preferred_element_type=F32)
    dq[here, :] = (dq_t.T * FACTOR).astype(BF16)


def fused(
    heads, blks, lists, q, k, v, g, oq, ok, ov,
    lq, lg, kv, skv, dq, dk, dv, dsk, dsv, bk, bv, sums, edges, block_sum, kt, skt, live, scores, gprob,
    send_in, recv_in, send_first, recv_first, send_own, send_sum, recv_sum, send_pass, recv_pass, send_halo,
    recv_halo, send_out, recv_out, keep_out, send_late, recv_late, keep_late, send_part, recv_part, send_edge,
    recv_edge,
):
    head, blk = lax.axis_index("head"), lax.axis_index("blk")
    part = q.shape[0]
    rows = heads * part
    keys = blks * QBLK
    rest = part - QBLK
    chips = blks // 2
    chip, core = blk // 2, lax.rem(blk, 2)
    sibling = blk + 1 - 2 * core
    lk, lv = kv.at[0], kv.at[1]
    sk, sv = skv.at[0], skv.at[1]

    arrays = ((k, lk, HALO), (v, lv, HALO), (q, lq, 0), (g, lg, 0))

    def into(which, source, there):
        src, dst, skip = arrays[which]
        return remote(
            src.at[:, aligned(there * DH, DH)],
            dst.at[aligned(skip + source * part, part)],
            send_in.at[which, there],
            recv_in.at[which, source],
            head=there,
        )

    def first(which, there):
        src, dst, _ = arrays[which]
        return remote(
            src.at[pl.ds(0, QBLK), aligned(there * DH, DH)],
            dst.at[pl.ds(HALO, QBLK)],
            send_first.at[which, there],
            recv_first.at[which],
            head=there,
        )

    def second(which, there):
        src, dst, _ = arrays[which]
        return remote(
            src.at[pl.ds(QBLK, rest), aligned(there * DH, DH)],
            dst.at[pl.ds(HALO + QBLK, rest)],
            send_in.at[which, there],
            recv_in.at[which, 0],
            head=there,
        )

    def own(which):
        src, dst, skip = arrays[which]
        return pltpu.make_async_copy(
            src.at[:, aligned(head * DH, DH)], dst.at[aligned(skip + head * part, part)], send_own.at[which]
        )

    def other(step):
        return lax.rem(head + step, heads)

    def slot(owner):
        return skv.at[:, aligned(owner * QBLK, QBLK)]

    def summary(owner, there):
        return remote(
            kv.at[:, pl.ds(HALO, QBLK)],
            slot(owner),
            send_sum.at[there],
            recv_sum.at[owner],
            blk=there * 2 + core,
        )

    def direct():
        return remote(kv.at[:, pl.ds(HALO, QBLK)], slot(chip * 2), send_pass.at[blks], recv_pass.at[blks], blk=sibling)

    def passed(owner):
        return remote(slot(owner), slot(owner), send_pass.at[owner], recv_pass.at[owner], blk=sibling)

    def halo(there):
        return remote(kv.at[:, pl.ds(rows, HALO)], kv.at[:, pl.ds(0, HALO)], send_halo, recv_halo, blk=there)

    def arrive(which, source):
        @pl.when(head != source)
        def _():
            if which < 2 and isinstance(source, int) and source == 0:
                second(which, head).wait_recv()
            else:
                into(which, source, head).wait_recv()

    greet(heads, blks)

    @pl.when(head == 0)
    def _():
        for step in range(1, heads):
            for which in range(2):
                first(which, step).start()

    for which in range(4):
        own(which).start()
    mark_live(lists, live)

    for which in range(2):
        own(which).wait()

        @pl.when(head > 0)
        def _():
            first(which, head).wait_recv()

    for there in range(1, chips):
        @pl.when(there > chip)
        def _():
            summary(blk, there).start()

    @pl.when(core == 0)
    def _():
        direct().start()

    @pl.when(head == 0)
    def _():
        for step in range(1, heads):
            for which in range(2):
                second(which, step).start()

    @pl.when(head > 0)
    def _():
        for step in range(1, heads):
            for which in range(2):
                into(which, head, other(step)).start()

    for ref in (dk, dv, dsk, dsv):
        ref[...] = jnp.zeros(ref.shape, ref.dtype)
    for owner in range(blks):
        @pl.when(owner > blk)
        def _():
            skv[:, pl.ds(owner * QBLK, QBLK), :] = jnp.zeros((2, QBLK, DH), BF16)

    skv[:, aligned(blk * QBLK, QBLK), :] = kv[:, pl.ds(HALO, QBLK), :]

    @pl.when(blk == 0)
    def _():
        kv[:, pl.ds(0, HALO), :] = jnp.zeros((2, HALO, DH), BF16)

    for there in range(chips - 1):
        @pl.when(there < chip)
        def _():
            summary(there * 2 + core, chip).wait_recv()
            passed(there * 2 + core).start()

    for source in range(heads - 1, -1, -1):
        for which in range(2):
            arrive(which, source)
        if source == heads - 2:
            @pl.when(blk + 1 < blks)
            def _():
                halo(blk + 1).start()

    @pl.when(head == 0)
    def _():
        for step in range(1, heads):
            for which in range(2):
                first(which, step).wait_send()
                second(which, step).wait_send()

    @pl.when(head > 0)
    def _():
        for step in range(1, heads):
            for which in range(2):
                into(which, head, other(step)).wait_send()

    for step in range(1, heads):
        for which in range(2, 4):
            into(which, head, other(step)).start()

    for start in range(HALO, HALO + rows, QBLK):
        kt[:, pl.ds(start, QBLK)] = lk[pl.ds(start, QBLK), :].T

    @pl.when(blk > 0)
    def _():
        halo(blk).wait_recv()

    for start in range(0, HALO, QBLK):
        kt[:, pl.ds(start, QBLK)] = lk[pl.ds(start, QBLK), :].T

    for there in range(chips - 1):
        @pl.when(there < chip)
        def _():
            passed(there * 2 + 1 - core).wait_recv()

    @pl.when(core == 1)
    def _():
        direct().wait_recv()

    for start in range(0, keys, QBLK):
        skt[:, pl.ds(start, QBLK)] = sk[pl.ds(start, QBLK), :].T
    for which in range(2, 4):
        own(which).wait()

    outs = ((dq, oq, 0), (bk, ok, HALO), (bv, ov, HALO))
    sets = ((dk, dsk, bk, FACTOR), (dv, dsv, bv, 1.0))

    def back(which, source, there):
        src, dst, skip = outs[which]
        return remote(
            src.at[aligned(skip + there * part, part)],
            dst.at[:, aligned(source * DH, DH)],
            send_out.at[which, there],
            recv_out.at[which, source],
            head=there,
        )

    def back_second(which, source):
        src, dst, skip = outs[which]
        return remote(
            src.at[pl.ds(skip + QBLK, rest)],
            dst.at[pl.ds(QBLK, rest), aligned(source * DH, DH)],
            send_out.at[which, 0],
            recv_out.at[which, source],
            head=0,
        )

    def back_first(which, source):
        src, dst, skip = outs[which]
        return remote(
            src.at[pl.ds(skip, QBLK)],
            dst.at[pl.ds(0, QBLK), aligned(source * DH, DH)],
            send_late.at[which],
            recv_late.at[which, source],
            head=0,
        )

    def keep(which):
        src, dst, skip = outs[which]
        return pltpu.make_async_copy(
            src.at[aligned(skip + head * part, part)], dst.at[:, aligned(head * DH, DH)], keep_out.at[which]
        )

    def keep_second(which):
        src, dst, skip = outs[which]
        return pltpu.make_async_copy(
            src.at[pl.ds(skip + QBLK, rest)], dst.at[pl.ds(QBLK, rest), pl.ds(0, DH)], keep_out.at[which]
        )

    def keep_first(which):
        src, dst, skip = outs[which]
        return pltpu.make_async_copy(
            src.at[pl.ds(skip, QBLK)], dst.at[pl.ds(0, QBLK), pl.ds(0, DH)], keep_late.at[which]
        )

    def send(which, there):
        @pl.when(head != there)
        def _():
            back(which, head, there).start()

        @pl.when(head == there)
        def _():
            keep(which).start()

    def partial(owner, source):
        return remote(
            sums.at[0, :, aligned(owner * QBLK, QBLK)],
            sums.at[1, :, aligned(source * QBLK, QBLK)],
            send_part.at[owner],
            recv_part.at[source],
            blk=owner,
        )

    def edge(there):
        return remote(edges.at[0], edges.at[1], send_edge, recv_edge, blk=there)

    def finish(there):
        at = aligned(HALO + there * part, part)
        for which in range(2):
            acc, _, out, scale = sets[which]
            out[at, :] = (acc[at, :] * scale).astype(BF16)
            send(1 + which, there)

    def finish_second():
        at = pl.ds(HALO + QBLK, rest)
        for which in range(2):
            acc, _, out, scale = sets[which]
            out[at, :] = (acc[at, :] * scale).astype(BF16)

            @pl.when(head > 0)
            def _():
                back_second(1 + which, head).start()

            @pl.when(head == 0)
            def _():
                keep_second(1 + which).start()

    def send_edges():
        @pl.when(blk > 0)
        def _():
            for which in range(2):
                acc, _, _, scale = sets[which]
                edges[0, which] = (acc[pl.ds(0, HALO), :] * scale).astype(BF16)
            edge(blk - 1).start()

    def finish_last():
        @pl.when(blk + 1 < blks)
        def _():
            edge(blk).wait_recv()
            for which in range(2):
                acc, _, _, scale = sets[which]
                acc[pl.ds(rows, HALO), :] += edges[1, which].astype(F32) * (1.0 / scale)

        for there in range(heads - 2, heads):
            finish(there)

    def step_of(step, carry):
        c = lax.rem(head - step + heads, heads)

        @pl.when(step > 0)
        def _():
            for which in range(2, 4):
                into(which, c, head).wait_recv()

        attend(c, lq, lk, lv, lg, sk, sv, dq, dk, dv, dsk, dsv, kt, skt, live, scores, gprob)
        send(0, c)

        @pl.when((step >= 2) & (c > 0) & (c < heads - 2))
        def _():
            finish(c)

        @pl.when((step >= 2) & (c == 0))
        def _():
            finish_second()

        @pl.when((step > 0) & (c == 0))
        def _():
            send_edges()

        @pl.when((step == head + 3) & (head > 0))
        def _():
            finish_last()

        return carry

    lax.fori_loop(0, heads, step_of, 0)

    for which in range(2):
        _, acc_sum, _, scale = sets[which]
        sums[0, which] = (acc_sum[...] * scale).astype(BF16)
    for owner in range(blks - 1):
        @pl.when(owner < blk)
        def _():
            partial(owner, blk).start()

    @pl.when(head == 0)
    def _():
        send_edges()

    for step in range(2):
        c = lax.rem(head - step + heads, heads)

        @pl.when((c > 0) & (c < heads - 2))
        def _():
            finish(c)

        @pl.when(c == 0)
        def _():
            finish_second()

    @pl.when((head == 0) | (head > heads - 4))
    def _():
        finish_last()

    for which in range(2):
        acc, acc_sum, _, scale = sets[which]
        block_sum[which] = (acc[pl.ds(HALO, QBLK), :] + acc_sum[aligned(blk * QBLK, QBLK), :]) * scale
    for source in range(1, blks):
        @pl.when(source > blk)
        def _():
            partial(blk, source).wait_recv()
            block_sum[...] += sums[1, :, pl.ds(source * QBLK, QBLK), :].astype(F32)

    for which in range(2):
        out = sets[which][2]
        out[pl.ds(HALO, QBLK), :] = block_sum[which].astype(BF16)

        @pl.when(head > 0)
        def _():
            back_first(1 + which, head).start()

        @pl.when(head == 0)
        def _():
            keep_first(1 + which).start()

    for step in range(1, heads):
        for which in range(2, 4):
            into(which, head, other(step)).wait_send()

    for there in range(1, chips):
        @pl.when(there > chip)
        def _():
            summary(blk, there).wait_send()

    @pl.when(core == 0)
    def _():
        direct().wait_send()

    for there in range(chips - 1):
        @pl.when(there < chip)
        def _():
            passed(there * 2 + core).wait_send()

    for owner in range(blks - 1):
        @pl.when(owner < blk)
        def _():
            partial(owner, blk).wait_send()

    @pl.when(blk + 1 < blks)
    def _():
        halo(blk + 1).wait_send()

    @pl.when(blk > 0)
    def _():
        edge(blk - 1).wait_send()

    keep(0).wait()
    for step in range(1, heads):
        back(0, head, other(step)).wait_send()
        back(0, other(step), head).wait_recv()

    @pl.when(head == 0)
    def _():
        for which in range(1, 3):
            keep_second(which).wait()
            keep_first(which).wait()
            for there in range(1, heads):
                back(which, 0, there).wait_send()
                back_second(which, there).wait_recv()
                back_first(which, there).wait_recv()

    @pl.when(head > 0)
    def _():
        for which in range(1, 3):
            keep(which).wait()
            back_second(which, head).wait_send()
            back_first(which, head).wait_send()
            for there in range(1, heads):
                @pl.when(there != head)
                def _():
                    back(which, head, there).wait_send()
            for step in range(1, heads):
                back(which, other(step), head).wait_recv()


def copy_kernel(x, y, z, ox, oy, oz, sem):
    copies = [pltpu.make_async_copy(a, b, sem.at[i]) for i, (a, b) in enumerate(((x, ox), (y, oy), (z, oz)))]
    for copy in copies:
        copy.start()
    for copy in copies:
        copy.wait()


def body_of(heads, blks):
    def body(queries, key_in, values, grad_out, block_list):
        part, width = queries.shape
        rows, keys = heads * part, blks * QBLK
        dma = pltpu.SemaphoreType.DMA
        whole = pl.BlockSpec(memory_space=VMEM)
        far = pl.BlockSpec(memory_space=pltpu.HBM)
        result = (jax.ShapeDtypeStruct((part, width), BF16),) * 3
        found = pl.pallas_call(
            lambda *refs: fused(heads, blks, *refs),
            out_shape=result,
            in_specs=[whole] + [far] * 4,
            out_specs=[far] * 3,
            scratch_shapes=[
                VMEM((rows, DH), BF16),
                VMEM((rows, DH), BF16),
                VMEM((2, HALO + rows, DH), BF16),
                VMEM((2, keys, DH), BF16),
                VMEM((rows, DH), BF16),
                VMEM((HALO + rows, DH), F32),
                VMEM((HALO + rows, DH), F32),
                VMEM((keys, DH), F32),
                VMEM((keys, DH), F32),
                VMEM((HALO + rows, DH), BF16),
                VMEM((HALO + rows, DH), BF16),
                VMEM((2, 2, keys, DH), BF16),
                VMEM((2, 2, HALO, DH), BF16),
                VMEM((2, QBLK, DH), F32),
                VMEM((DH, HALO + rows), BF16),
                VMEM((DH, keys), BF16),
                VMEM((rows // CHUNK, SEGB, CHUNK), F32),
                VMEM((keys + WIDE, CHUNK), F32),
                VMEM((keys + WIDE, CHUNK), F32),
                dma((4, heads)),
                dma((4, heads)),
                dma((2, heads)),
                dma((2,)),
                dma((4,)),
                dma((blks // 2,)),
                dma((blks,)),
                dma((blks + 1,)),
                dma((blks + 1,)),
                dma,
                dma,
                dma((3, heads)),
                dma((3, heads)),
                dma((3,)),
                dma((3,)),
                dma((3, heads)),
                dma((3,)),
                dma((blks,)),
                dma((blks,)),
                dma,
                dma,
            ],
            compiler_params=pltpu.CompilerParams(
                collective_id=0, has_side_effects=True, vmem_limit_bytes=62 * 1024 * 1024
            ),
            name="attention_backward",
        )(block_list.T, queries, key_in, values, grad_out)
        return pl.pallas_call(
            copy_kernel,
            out_shape=result,
            in_specs=[far] * 3,
            out_specs=[far] * 3,
            scratch_shapes=[dma((3,))],
            name="results",
        )(*found)

    return body


def solution(mesh):
    placed = P(("blk", "head"), None)
    return jax.shard_map(
        body_of(mesh.shape["head"], mesh.shape["blk"]),
        mesh=mesh,
        in_specs=(placed,) * 4 + (P(),),
        out_specs=(placed,) * 3,
        check_vma=False,
    )
```

```python
import functools
import math

import jax
import jax.numpy as jnp
from jax import lax
from jax.experimental import pallas as pl
from jax.experimental.pallas import tpu as pltpu
from jax.sharding import PartitionSpec as P

DH = 128
QBLK = 128
MAXB = 16
SEGB = 16
HALO = 3 * QBLK
CHUNK = 2 * QBLK
WIDE = HALO + CHUNK
EARLY = 2
MESH = pl.DeviceIdType.MESH
VMEM = pltpu.VMEM
BF16 = jnp.bfloat16
F32 = jnp.float32
DEAD = -3e38
FACTOR = 1.0 / math.sqrt(DH)
NT = (((1,), (1,)), ((), ()))
TN = (((0,), (0,)), ((), ()))


def aligned(start, size):
    return pl.ds(pl.multiple_of(start, QBLK), size)


def remote(src, dst, send, recv, **where):
    return pltpu.make_async_remote_copy(
        src_ref=src,
        dst_ref=dst,
        send_sem=send,
        recv_sem=recv,
        device_id=where,
        device_id_type=MESH,
    )


def greet(heads, blks):
    head, blk = lax.axis_index("head"), lax.axis_index("blk")
    core = lax.rem(blk, 2)
    barrier = pltpu.get_barrier_semaphore()

    def signal(**where):
        pl.semaphore_signal(barrier, inc=1, device_id=where, device_id_type=MESH)

    for step in range(1, heads):
        signal(head=lax.rem(head + step, heads))
    for step in range(2, blks, 2):
        signal(blk=lax.rem(blk + step, blks))
    signal(blk=blk + 1 - 2 * core)
    near = blk - 1 + 2 * core
    has_near = (near >= 0) & (near < blks)

    @pl.when(has_near)
    def _():
        signal(blk=near)

    pl.semaphore_wait(barrier, heads - 1 + blks // 2 + has_near.astype(jnp.int32))


def mark_live(lists, live):
    blk = lax.axis_index("blk")
    blocks = lists.shape[1]
    chips = SEGB // 2

    def owner_of(shape):
        slot = lax.broadcasted_iota(jnp.int32, shape, 0)
        return 2 * lax.rem(slot, chips) + slot // chips

    owner = owner_of((SEGB, blocks))
    seen = jnp.zeros((SEGB, blocks), F32)
    for entry in range(MAXB):
        seen = jnp.where(lists[entry : entry + 1, :] == owner * SEGB, 1.0, seen)
    column = lax.broadcasted_iota(jnp.int32, (blocks, CHUNK), 0)
    query = lax.broadcasted_iota(jnp.int32, (blocks, CHUNK), 1) // QBLK
    slot = owner_of((SEGB, CHUNK)) * SEGB
    reader = lax.broadcasted_iota(jnp.int32, (SEGB, CHUNK), 1) // QBLK
    for c in range(live.shape[0]):
        first = blk * SEGB + 2 * c
        spread = jnp.where(column == query + first, 1.0, 0.0).astype(BF16)
        chosen = jnp.dot(seen.astype(BF16), spread, preferred_element_type=F32)
        live[c] = jnp.where(slot < reader + (first - 3), chosen, 0.0)


def attend(c, pairs, q, k, v, g, sk, sv, dq, dk, dv, dsk, dsv, live, scores, gprob):
    blk = lax.axis_index("blk")
    keys = sk.shape[0]
    exp2_factor = FACTOR * math.log2(math.e)
    starts = [half + s * CHUNK for half in (0, keys // 2) for s in range(pairs)]
    base = pl.multiple_of(c * CHUNK, CHUNK)
    here = pl.ds(base, CHUNK)
    window = pl.ds(base, WIDE)
    queries, grads = q[here, :], g[here, :]
    slabs = [(pl.ds(s, CHUNK), pl.ds(s, CHUNK), sk, sv, dsk, dsv) for s in starts]
    slabs.append((pl.ds(keys, WIDE), window, k, v, dk, dv))

    tops, totals, dots = [], [], []
    for (at, rows, keys_of, values_of, _, _), start in zip(slabs, starts + [None]):
        raw = lax.dot_general(keys_of[rows, :], queries, NT, preferred_element_type=F32) * exp2_factor
        gp = lax.dot_general(values_of[rows, :], grads, NT, preferred_element_type=F32)
        if start is None:
            key_row = lax.broadcasted_iota(jnp.int32, (WIDE, CHUNK), 0)
            query_row = lax.broadcasted_iota(jnp.int32, (WIDE, CHUNK), 1)
            alive = (
                (key_row <= query_row + HALO)
                & ((key_row >= QBLK) | (query_row < QBLK))
                & ((blk > 0) | (key_row + base >= HALO))
            )
            masked = jnp.where(alive, raw, DEAD)
        else:
            masked = jnp.concatenate(
                [
                    jnp.where(live[c, pl.ds((start + sub) // QBLK, 1), :] > 0.5, raw[sub : sub + QBLK], DEAD)
                    for sub in range(0, CHUNK, QBLK)
                ],
                axis=0,
            )
        top = jnp.max(masked, axis=0, keepdims=True)
        weight = jnp.exp2(masked - top)
        scores[at, :] = weight
        gprob[at, :] = gp
        tops.append(top)
        totals.append(jnp.sum(weight, axis=0, keepdims=True))
        dots.append(jnp.sum(weight * gp, axis=0, keepdims=True))

    top = functools.reduce(jnp.maximum, tops)
    shares = [jnp.exp2(t - top) for t in tops]
    total = sum(t * share for t, share in zip(totals, shares))
    inverse = 1.0 / total
    row_dot = sum(t * share for t, share in zip(dots, shares)) * inverse

    query_grad = jnp.zeros((CHUNK, DH), F32)
    for (at, rows, keys_of, _, dk_of, dv_of), share in zip(slabs, shares):
        prob = scores[at, :] * (share * inverse)
        ds = (prob * (gprob[at, :] - row_dot)).astype(BF16)
        dv_of[rows, :] += jnp.dot(prob.astype(BF16), grads, preferred_element_type=F32)
        dk_of[rows, :] += jnp.dot(ds, queries, preferred_element_type=F32)
        query_grad += lax.dot_general(ds, keys_of[rows, :], TN, preferred_element_type=F32)
    dq[here, :] = (query_grad * FACTOR).astype(BF16)


def fused(
    heads, blks, lists, q, k, v, g, oq, ok, ov,
    lq, lg, kv, skv, dq, dk, dv, dsk, dsv, bk, bv, hand, sums, edges, block_sum, live, scores, gprob,
    send_in, recv_in, send_first, recv_first, send_own, send_sum, recv_sum, send_pass, recv_pass, send_halo,
    recv_halo, send_out, recv_out, keep_out, send_late, recv_late, keep_late, send_hand, recv_hand, send_part,
    recv_part, send_edge, recv_edge,
):
    head, blk = lax.axis_index("head"), lax.axis_index("blk")
    part = q.shape[0]
    rows = heads * part
    keys = blks * QBLK
    rest = part - QBLK
    chips = blks // 2
    chip, core = blk // 2, lax.rem(blk, 2)
    sibling = blk + 1 - 2 * core
    lk, lv = kv.at[0], kv.at[1]
    sk, sv = skv.at[0], skv.at[1]

    arrays = ((k, lk, HALO), (v, lv, HALO), (q, lq, 0), (g, lg, 0))

    def into(which, source, there):
        src, dst, skip = arrays[which]
        return remote(
            src.at[:, aligned(there * DH, DH)],
            dst.at[aligned(skip + source * part, part)],
            send_in.at[which, there],
            recv_in.at[which, source],
            head=there,
        )

    def first(which, there):
        src, dst, _ = arrays[which]
        return remote(
            src.at[pl.ds(0, QBLK), aligned(there * DH, DH)],
            dst.at[pl.ds(HALO, QBLK)],
            send_first.at[which, there],
            recv_first.at[which],
            head=there,
        )

    def second(which, there):
        src, dst, _ = arrays[which]
        return remote(
            src.at[pl.ds(QBLK, rest), aligned(there * DH, DH)],
            dst.at[pl.ds(HALO + QBLK, rest)],
            send_in.at[which, there],
            recv_in.at[which, 0],
            head=there,
        )

    def own(which):
        src, dst, skip = arrays[which]
        return pltpu.make_async_copy(
            src.at[:, aligned(head * DH, DH)], dst.at[aligned(skip + head * part, part)], send_own.at[which]
        )

    def other(step):
        return lax.rem(head + step, heads)

    def chunk_at(step):
        return lax.rem(head - step + heads, heads)

    place = chunk_at

    def done_at(c):
        late = jnp.maximum(place(c), place(jnp.minimum(c + 1, heads - 1)))
        return jnp.maximum(late, place(jnp.minimum(c + 2, heads - 1)))

    def slot(place_of, of_chip):
        return skv.at[:, aligned((place_of * chips + of_chip) * QBLK, QBLK)]

    def summary(of_chip, there):
        return remote(
            kv.at[:, pl.ds(HALO, QBLK)],
            slot(core, of_chip),
            send_sum.at[there],
            recv_sum.at[of_chip],
            blk=there * 2 + core,
        )

    def direct():
        return remote(
            kv.at[:, pl.ds(HALO, QBLK)], slot(0, chip), send_pass.at[chips], recv_pass.at[chips], blk=sibling
        )

    def passed(place_of, of_chip):
        return remote(
            slot(place_of, of_chip), slot(place_of, of_chip), send_pass.at[of_chip], recv_pass.at[of_chip], blk=sibling
        )

    def halo(there):
        return remote(kv.at[:, pl.ds(rows, HALO)], kv.at[:, pl.ds(0, HALO)], send_halo, recv_halo, blk=there)

    def arrive(which, source):
        @pl.when(head != source)
        def _():
            if which < 2 and isinstance(source, int) and source == 0:
                second(which, head).wait_recv()
            else:
                into(which, source, head).wait_recv()

    def drain_keys():
        @pl.when(head == 0)
        def _():
            for step in range(1, heads):
                for which in range(2):
                    first(which, step).wait_send()
                    second(which, step).wait_send()

        @pl.when(head > 0)
        def _():
            for step in range(1, heads):
                for which in range(2):
                    into(which, head, other(step)).wait_send()

    def drain_queries():
        for step in range(1, heads):
            for which in range(2, 4):
                into(which, head, other(step)).wait_send()

    def drain_summary():
        for there in range(1, chips):
            @pl.when(there > chip)
            def _():
                summary(chip, there).wait_send()

        @pl.when(core == 0)
        def _():
            direct().wait_send()

        for there in range(chips - 1):
            @pl.when(there < chip)
            def _():
                passed(core, there).wait_send()

        @pl.when(blk + 1 < blks)
        def _():
            halo(blk + 1).wait_send()

    greet(heads, blks)

    for which in range(4):
        own(which).start()

    @pl.when(head == 0)
    def _():
        for which in range(2):
            for step in range(1, heads):
                first(which, step).start()

    def send_keys(which):
        @pl.when(head == 0)
        def _():
            for step in range(1, heads):
                second(which, step).start()

        @pl.when(head > 0)
        def _():
            for step in range(1, heads):
                into(which, head, other(step)).start()

    send_keys(0)
    mark_live(lists, live)

    for which in range(2):
        own(which).wait()

        @pl.when(head > 0)
        def _():
            first(which, head).wait_recv()

    @pl.when(core == 0)
    def _():
        direct().start()

    for there in range(1, chips):
        @pl.when(there > chip)
        def _():
            summary(chip, there).start()

    send_keys(1)
    for step in range(1, 1 + EARLY):
        for which in range(2, 4):
            into(which, head, other(step)).start()

    for ref in (dk, dv, dsk, dsv):
        ref[...] = jnp.zeros(ref.shape, ref.dtype)
    nothing = jnp.zeros((2, QBLK, DH), BF16)
    for there in range(1, chips):
        @pl.when(there > chip)
        def _():
            for half in range(2):
                skv[:, pl.ds((half * chips + there) * QBLK, QBLK), :] = nothing

    @pl.when(core == 0)
    def _():
        skv[:, aligned((chips + chip) * QBLK, QBLK), :] = nothing

    skv[:, aligned((core * chips + chip) * QBLK, QBLK), :] = kv[:, pl.ds(HALO, QBLK), :]

    @pl.when(blk == 0)
    def _():
        kv[:, pl.ds(0, HALO), :] = jnp.zeros((2, HALO, DH), BF16)

    for there in range(chips - 1):
        @pl.when(there < chip)
        def _():
            summary(there, chip).wait_recv()
            passed(core, there).start()

    for source in range(heads - 1, -1, -1):
        for which in range(2):
            arrive(which, source)
        if source == heads - 2:
            @pl.when(blk + 1 < blks)
            def _():
                halo(blk + 1).start()

    drain_keys()
    for step in range(1 + EARLY, heads):
        for which in range(2, 4):
            into(which, head, other(step)).start()

    @pl.when(blk > 0)
    def _():
        halo(blk).wait_recv()

    for there in range(chips - 1):
        @pl.when(there < chip)
        def _():
            passed(1 - core, there).wait_recv()

    @pl.when(core == 1)
    def _():
        direct().wait_recv()

    for which in range(2, 4):
        own(which).wait()

    outs = ((dq, oq, 0), (bk, ok, HALO), (bv, ov, HALO))
    sets = ((dk, dsk, bk, FACTOR), (dv, dsv, bv, 1.0))

    def back(which, source, there):
        src, dst, skip = outs[which]
        return remote(
            src.at[aligned(skip + there * part, part)],
            dst.at[:, aligned(source * DH, DH)],
            send_out.at[which, there],
            recv_out.at[which, source],
            head=there,
        )

    def back_second(which, source):
        src, dst, skip = outs[which]
        return remote(
            src.at[pl.ds(skip + QBLK, rest)],
            dst.at[pl.ds(QBLK, rest), aligned(source * DH, DH)],
            send_out.at[which, 0],
            recv_out.at[which, source],
            head=0,
        )

    def back_first(which, source):
        src, dst, skip = outs[which]
        return remote(
            src.at[pl.ds(skip, QBLK)],
            dst.at[pl.ds(0, QBLK), aligned(source * DH, DH)],
            send_late.at[which],
            recv_late.at[which, source],
            head=0,
        )

    def keep(which):
        src, dst, skip = outs[which]
        return pltpu.make_async_copy(
            src.at[aligned(skip + head * part, part)], dst.at[:, aligned(head * DH, DH)], keep_out.at[which]
        )

    def keep_second(which):
        src, dst, skip = outs[which]
        return pltpu.make_async_copy(
            src.at[pl.ds(skip + QBLK, rest)], dst.at[pl.ds(QBLK, rest), pl.ds(0, DH)], keep_out.at[which]
        )

    def keep_first(which):
        src, dst, skip = outs[which]
        return pltpu.make_async_copy(
            src.at[pl.ds(skip, QBLK)], dst.at[pl.ds(0, QBLK), pl.ds(0, DH)], keep_late.at[which]
        )

    def send(which, there):
        @pl.when(head != there)
        def _():
            back(which, head, there).start()

        @pl.when(head == there)
        def _():
            keep(which).start()

    def handed():
        return remote(hand.at[0], hand.at[1], send_hand, recv_hand, blk=sibling)

    def partial(owner, source):
        return remote(
            sums.at[0, :, aligned(owner * QBLK, QBLK)],
            sums.at[1, :, aligned(source * QBLK, QBLK)],
            send_part.at[owner],
            recv_part.at[source],
            blk=owner * 2 + core,
        )

    def edge(there):
        return remote(edges.at[0], edges.at[1], send_edge, recv_edge, blk=there)

    def finish(there):
        at = aligned(HALO + there * part, part)
        for which in range(2):
            acc, _, out, scale = sets[which]
            out[at, :] = (acc[at, :] * scale).astype(BF16)
            send(1 + which, there)

    def finish_second():
        at = pl.ds(HALO + QBLK, rest)
        for which in range(2):
            acc, _, out, scale = sets[which]
            out[at, :] = (acc[at, :] * scale).astype(BF16)

            @pl.when(head > 0)
            def _():
                back_second(1 + which, head).start()

            @pl.when(head == 0)
            def _():
                keep_second(1 + which).start()

    def send_edges():
        @pl.when(blk > 0)
        def _():
            for which in range(2):
                acc, _, _, scale = sets[which]
                edges[0, which] = (acc[pl.ds(0, HALO), :] * scale).astype(BF16)
            edge(blk - 1).start()

    def finish_last():
        @pl.when(blk + 1 < blks)
        def _():
            edge(blk).wait_recv()
            for which in range(2):
                acc, _, _, scale = sets[which]
                acc[pl.ds(rows, HALO), :] += edges[1, which].astype(F32) * (1.0 / scale)

        for there in range(heads - 2, heads):
            finish(there)

    edges_at = jnp.maximum(place(0), place(1))
    last_at = jnp.maximum(edges_at + 2, jnp.maximum(place(heads - 2), place(heads - 1)))

    def step_of(step, carry):
        c = chunk_at(step)

        @pl.when(step > 0)
        def _():
            for which in range(2, 4):
                into(which, c, head).wait_recv()

        for pairs in range(1, chips // 2 + 1):
            @pl.when(chip // 2 + 1 == pairs)
            def _():
                attend(c, pairs, lq, lk, lv, lg, sk, sv, dq, dk, dv, dsk, dsv, live, scores, gprob)

        send(0, c)

        for back_by in range(3):
            ready = c - back_by

            @pl.when((ready > 0) & (ready < heads - 2) & (done_at(ready) == step))
            def _():
                finish(ready)

        @pl.when(done_at(0) == step)
        def _():
            finish_second()

        @pl.when(edges_at == step)
        def _():
            send_edges()

        @pl.when(last_at == step)
        def _():
            finish_last()

        return carry

    lax.fori_loop(0, heads, step_of, 0)

    half = chips * QBLK
    for which in range(2):
        _, acc_sum, _, scale = sets[which]
        hand[0, which] = (acc_sum[aligned((1 - core) * half, half), :] * scale).astype(BF16)
    handed().start()
    handed().wait_recv()
    for which in range(2):
        acc, acc_sum, _, scale = sets[which]
        for there in range(chips - 1):
            @pl.when(there < chip)
            def _():
                at = pl.ds(there * QBLK, QBLK)
                mine = acc_sum[aligned(core * half + there * QBLK, QBLK), :] * scale
                sums[0, which, at, :] = (mine + hand[1, which, at, :].astype(F32)).astype(BF16)

    for there in range(chips - 1):
        @pl.when(there < chip)
        def _():
            partial(there, chip).start()

    @pl.when(last_at >= heads)
    def _():
        finish_last()

    for which in range(2):
        acc, acc_sum, _, scale = sets[which]
        at = aligned(chip * QBLK, QBLK)
        mine = acc[pl.ds(HALO, QBLK), :] + acc_sum[aligned(core * half + chip * QBLK, QBLK), :]
        block_sum[which] = mine * scale + hand[1, which, at, :].astype(F32)
    for source in range(chips - 1, 0, -1):
        @pl.when(source > chip)
        def _():
            partial(chip, source).wait_recv()
            block_sum[...] += sums[1, :, pl.ds(source * QBLK, QBLK), :].astype(F32)

    for which in range(2):
        out = sets[which][2]
        out[pl.ds(HALO, QBLK), :] = block_sum[which].astype(BF16)

        @pl.when(head > 0)
        def _():
            back_first(1 + which, head).start()

        @pl.when(head == 0)
        def _():
            keep_first(1 + which).start()

    drain_queries()
    drain_summary()
    handed().wait_send()
    for there in range(chips - 1):
        @pl.when(there < chip)
        def _():
            partial(there, chip).wait_send()

    @pl.when(blk > 0)
    def _():
        edge(blk - 1).wait_send()

    keep(0).wait()
    for step in range(1, heads):
        back(0, head, other(step)).wait_send()
        back(0, other(step), head).wait_recv()

    @pl.when(head == 0)
    def _():
        for which in range(1, 3):
            keep_second(which).wait()
            keep_first(which).wait()
            for there in range(1, heads):
                back(which, 0, there).wait_send()
                back_second(which, there).wait_recv()
                back_first(which, there).wait_recv()

    @pl.when(head > 0)
    def _():
        for which in range(1, 3):
            keep(which).wait()
            back_second(which, head).wait_send()
            back_first(which, head).wait_send()
            for there in range(1, heads):
                @pl.when(there != head)
                def _():
                    back(which, head, there).wait_send()
            for step in range(1, heads):
                back(which, other(step), head).wait_recv()


def body_of(heads, blks):
    def body(queries, key_in, values, grad_out, block_list):
        part, width = queries.shape
        rows, keys = heads * part, blks * QBLK
        dma = pltpu.SemaphoreType.DMA
        whole = pl.BlockSpec(memory_space=VMEM)
        far = pl.BlockSpec(memory_space=pltpu.HBM)
        result = (jax.ShapeDtypeStruct((part, width), BF16),) * 3
        return pl.pallas_call(
            lambda *refs: fused(heads, blks, *refs),
            out_shape=result,
            in_specs=[whole] + [far] * 4,
            out_specs=[whole] * 3,
            scratch_shapes=[
                VMEM((rows, DH), BF16),
                VMEM((rows, DH), BF16),
                VMEM((2, HALO + rows, DH), BF16),
                VMEM((2, keys, DH), BF16),
                VMEM((rows, DH), BF16),
                VMEM((HALO + rows, DH), F32),
                VMEM((HALO + rows, DH), F32),
                VMEM((keys, DH), F32),
                VMEM((keys, DH), F32),
                VMEM((HALO + rows, DH), BF16),
                VMEM((HALO + rows, DH), BF16),
                VMEM((2, 2, keys // 2, DH), BF16),
                VMEM((2, 2, keys // 2, DH), BF16),
                VMEM((2, 2, HALO, DH), BF16),
                VMEM((2, QBLK, DH), F32),
                VMEM((rows // CHUNK, SEGB, CHUNK), F32),
                VMEM((keys + WIDE, CHUNK), F32),
                VMEM((keys + WIDE, CHUNK), F32),
                dma((4, heads)),
                dma((4, heads)),
                dma((2, heads)),
                dma((2,)),
                dma((4,)),
                dma((blks // 2,)),
                dma((blks // 2,)),
                dma((blks // 2 + 1,)),
                dma((blks // 2 + 1,)),
                dma,
                dma,
                dma((3, heads)),
                dma((3, heads)),
                dma((3,)),
                dma((3,)),
                dma((3, heads)),
                dma((3,)),
                dma,
                dma,
                dma((blks // 2,)),
                dma((blks // 2,)),
                dma,
                dma,
            ],
            compiler_params=pltpu.CompilerParams(
                collective_id=0, has_side_effects=True, vmem_limit_bytes=62 * 1024 * 1024
            ),
            name="attention_backward",
        )(block_list.T, queries, key_in, values, grad_out)

    return body


def solution(mesh):
    placed = P(("blk", "head"), None)
    return jax.shard_map(
        body_of(mesh.shape["head"], mesh.shape["blk"]),
        mesh=mesh,
        in_specs=(placed,) * 4 + (P(),),
        out_specs=(placed,) * 3,
        check_vma=False,
    )
```

```python
import functools
import math

import jax
import jax.numpy as jnp
from jax import lax
from jax.experimental import pallas as pl
from jax.experimental.pallas import tpu as pltpu
from jax.sharding import PartitionSpec as P

DH = 128
QBLK = 128
MAXB = 16
SEGB = 16
HALO = 3 * QBLK
CHUNK = 2 * QBLK
WIDE = HALO + CHUNK
MESH = pl.DeviceIdType.MESH
VMEM = pltpu.VMEM
BF16 = jnp.bfloat16
F32 = jnp.float32
DEAD = -3e38
FACTOR = 1.0 / math.sqrt(DH)
NT = (((1,), (1,)), ((), ()))
TN = (((0,), (0,)), ((), ()))


def aligned(start, size):
    return pl.ds(pl.multiple_of(start, QBLK), size)


def remote(src, dst, send, recv, **where):
    return pltpu.make_async_remote_copy(
        src_ref=src,
        dst_ref=dst,
        send_sem=send,
        recv_sem=recv,
        device_id=where,
        device_id_type=MESH,
    )


def greet(heads, blks):
    head, blk = lax.axis_index("head"), lax.axis_index("blk")
    core = lax.rem(blk, 2)
    barrier = pltpu.get_barrier_semaphore()

    def signal(**where):
        pl.semaphore_signal(barrier, inc=1, device_id=where, device_id_type=MESH)

    for step in range(1, heads):
        signal(head=lax.rem(head + step, heads))
    for step in range(2, blks, 2):
        signal(blk=lax.rem(blk + step, blks))
    signal(blk=blk + 1 - 2 * core)
    near = blk - 1 + 2 * core
    has_near = (near >= 0) & (near < blks)

    @pl.when(has_near)
    def _():
        signal(blk=near)

    pl.semaphore_wait(barrier, heads - 1 + blks // 2 + has_near.astype(jnp.int32))


def mark_live(lists, live):
    blk = lax.axis_index("blk")
    blocks = lists.shape[1]
    chips = SEGB // 2

    def owner_of(shape):
        slot = lax.broadcasted_iota(jnp.int32, shape, 0)
        return 2 * lax.rem(slot, chips) + slot // chips

    owner = owner_of((SEGB, blocks))
    seen = jnp.zeros((SEGB, blocks), F32)
    for entry in range(MAXB):
        seen = jnp.where(lists[entry : entry + 1, :] == owner * SEGB, 1.0, seen)
    column = lax.broadcasted_iota(jnp.int32, (blocks, CHUNK), 0)
    query = lax.broadcasted_iota(jnp.int32, (blocks, CHUNK), 1) // QBLK
    slot = owner_of((SEGB, CHUNK)) * SEGB
    reader = lax.broadcasted_iota(jnp.int32, (SEGB, CHUNK), 1) // QBLK
    for c in range(live.shape[0]):
        first = blk * SEGB + 2 * c
        spread = jnp.where(column == query + first, 1.0, 0.0).astype(BF16)
        chosen = jnp.dot(seen.astype(BF16), spread, preferred_element_type=F32)
        live[c] = jnp.where(slot < reader + (first - 3), chosen, 0.0)


def attend(c, pairs, ready, summed, q, k, v, g, sk, sv, dq, dk, dv, dsk, dsv, live, scores, gprob):
    blk = lax.axis_index("blk")
    keys = sk.shape[0]
    exp2_factor = FACTOR * math.log2(math.e)
    starts = [half + s * CHUNK for half in (0, keys // 2) for s in range(pairs)]
    base = pl.multiple_of(c * CHUNK, CHUNK)
    here = pl.ds(base, CHUNK)
    window = pl.ds(base, WIDE)
    queries, grads = q[here, :], g[here, :]
    slabs = [(pl.ds(s, CHUNK), pl.ds(s, CHUNK), sk, sv, dsk, dsv) for s in starts]
    slabs.append((pl.ds(keys, WIDE), window, k, v, dk, dv))

    tops, totals, dots = [], [], []
    for (at, rows, keys_of, values_of, _, _), start in zip(slabs, starts + [None]):
        if start is None:
            ready()
        raw = lax.dot_general(keys_of[rows, :], queries, NT, preferred_element_type=F32) * exp2_factor
        gp = lax.dot_general(values_of[rows, :], grads, NT, preferred_element_type=F32)
        if start is None:
            key_row = lax.broadcasted_iota(jnp.int32, (WIDE, CHUNK), 0)
            query_row = lax.broadcasted_iota(jnp.int32, (WIDE, CHUNK), 1)
            alive = (
                (key_row <= query_row + HALO)
                & ((key_row >= QBLK) | (query_row < QBLK))
                & ((blk > 0) | (key_row + base >= HALO))
            )
            masked = jnp.where(alive, raw, DEAD)
        else:
            masked = jnp.concatenate(
                [
                    jnp.where(live[c, pl.ds((start + sub) // QBLK, 1), :] > 0.5, raw[sub : sub + QBLK], DEAD)
                    for sub in range(0, CHUNK, QBLK)
                ],
                axis=0,
            )
        top = jnp.max(masked, axis=0, keepdims=True)
        weight = jnp.exp2(masked - top)
        scores[at, :] = weight
        gprob[at, :] = gp
        tops.append(top)
        totals.append(jnp.sum(weight, axis=0, keepdims=True))
        dots.append(jnp.sum(weight * gp, axis=0, keepdims=True))

    top = functools.reduce(jnp.maximum, tops)
    shares = [jnp.exp2(t - top) for t in tops]
    total = sum(t * share for t, share in zip(totals, shares))
    inverse = 1.0 / total
    row_dot = sum(t * share for t, share in zip(dots, shares)) * inverse

    query_grad = jnp.zeros((CHUNK, DH), F32)
    for (at, rows, keys_of, _, dk_of, dv_of), share in zip(slabs, shares):
        if keys_of is k:
            summed()
        prob = scores[at, :] * (share * inverse)
        ds = (prob * (gprob[at, :] - row_dot)).astype(BF16)
        dv_of[rows, :] += jnp.dot(prob.astype(BF16), grads, preferred_element_type=F32)
        dk_of[rows, :] += jnp.dot(ds, queries, preferred_element_type=F32)
        query_grad += lax.dot_general(ds, keys_of[rows, :], TN, preferred_element_type=F32)
    dq[here, :] = (query_grad * FACTOR).astype(BF16)


def fused(
    heads, blks, lists, q, k, v, g, oq, ok, ov,
    lq, lg, kv, skv, dq, dk, dv, dsk, dsv, bk, bv, hand, sums, edges, block_sum, live, scores, gprob,
    send_in, recv_in, send_first, recv_first, send_own, send_sum, recv_sum, send_pass, recv_pass, send_halo,
    recv_halo, send_out, recv_out, keep_out, send_late, recv_late, keep_late, send_hand, recv_hand, send_part,
    recv_part, send_edge, recv_edge,
):
    head, blk = lax.axis_index("head"), lax.axis_index("blk")
    part = q.shape[0]
    rows = heads * part
    keys = blks * QBLK
    rest = part - QBLK
    chips = blks // 2
    chip, core = blk // 2, lax.rem(blk, 2)
    sibling = blk + 1 - 2 * core
    lk, lv = kv.at[0], kv.at[1]
    sk, sv = skv.at[0], skv.at[1]

    arrays = ((k, lk, HALO), (v, lv, HALO), (q, lq, 0), (g, lg, 0))

    def into(which, source, there):
        src, dst, skip = arrays[which]
        return remote(
            src.at[:, aligned(there * DH, DH)],
            dst.at[aligned(skip + source * part, part)],
            send_in.at[which, there],
            recv_in.at[which, source],
            head=there,
        )

    def first(which, there):
        src, dst, _ = arrays[which]
        return remote(
            src.at[pl.ds(0, QBLK), aligned(there * DH, DH)],
            dst.at[pl.ds(HALO, QBLK)],
            send_first.at[which, there],
            recv_first.at[which],
            head=there,
        )

    def second(which, there):
        src, dst, _ = arrays[which]
        return remote(
            src.at[pl.ds(QBLK, rest), aligned(there * DH, DH)],
            dst.at[pl.ds(HALO + QBLK, rest)],
            send_in.at[which, there],
            recv_in.at[which, 0],
            head=there,
        )

    def own(which):
        src, dst, skip = arrays[which]
        return pltpu.make_async_copy(
            src.at[:, aligned(head * DH, DH)], dst.at[aligned(skip + head * part, part)], send_own.at[which]
        )

    def other(step):
        return lax.rem(head + step, heads)

    def chunk_at(step):
        return lax.rem(head - step + heads, heads)

    place = chunk_at

    def done_at(c):
        late = jnp.maximum(place(c), place(jnp.minimum(c + 1, heads - 1)))
        return jnp.maximum(late, place(jnp.minimum(c + 2, heads - 1)))

    def slot(place_of, of_chip):
        return skv.at[:, aligned((place_of * chips + of_chip) * QBLK, QBLK)]

    def summary(of_chip, there):
        return remote(
            kv.at[:, pl.ds(HALO, QBLK)],
            slot(core, of_chip),
            send_sum.at[there],
            recv_sum.at[of_chip],
            blk=there * 2 + core,
        )

    def direct():
        return remote(
            kv.at[:, pl.ds(HALO, QBLK)], slot(0, chip), send_pass.at[chips], recv_pass.at[chips], blk=sibling
        )

    def passed(place_of, of_chip):
        return remote(
            slot(place_of, of_chip), slot(place_of, of_chip), send_pass.at[of_chip], recv_pass.at[of_chip], blk=sibling
        )

    def halo(there):
        return remote(kv.at[:, pl.ds(rows, HALO)], kv.at[:, pl.ds(0, HALO)], send_halo, recv_halo, blk=there)

    def arrive(which, source):
        @pl.when(head != source)
        def _():
            if which < 2 and isinstance(source, int) and source == 0:
                second(which, head).wait_recv()
            else:
                into(which, source, head).wait_recv()

    def drain_keys():
        @pl.when(head == 0)
        def _():
            for step in range(1, heads):
                for which in range(2):
                    first(which, step).wait_send()
                    second(which, step).wait_send()

        @pl.when(head > 0)
        def _():
            for step in range(1, heads):
                for which in range(2):
                    into(which, head, other(step)).wait_send()

    def drain_queries():
        for step in range(1, heads):
            for which in range(2, 4):
                into(which, head, other(step)).wait_send()

    def drain_summary():
        for there in range(1, chips):
            @pl.when(there > chip)
            def _():
                summary(chip, there).wait_send()

        @pl.when(core == 0)
        def _():
            direct().wait_send()

        for there in range(chips - 1):
            @pl.when(there < chip)
            def _():
                passed(core, there).wait_send()

        @pl.when(blk + 1 < blks)
        def _():
            halo(blk + 1).wait_send()

    greet(heads, blks)

    for which in range(4):
        own(which).start()

    @pl.when(head == 0)
    def _():
        for which in range(2):
            for step in range(1, heads):
                first(which, step).start()

    def send_keys(which):
        @pl.when(head == 0)
        def _():
            for step in range(1, heads):
                second(which, step).start()

        @pl.when(head > 0)
        def _():
            for step in range(1, heads):
                into(which, head, other(step)).start()

    send_keys(0)
    mark_live(lists, live)

    for which in range(2):
        own(which).wait()

        @pl.when(head > 0)
        def _():
            first(which, head).wait_recv()

    @pl.when(core == 0)
    def _():
        direct().start()

    for there in range(1, chips):
        @pl.when(there > chip)
        def _():
            summary(chip, there).start()

    send_keys(1)

    for ref in (dk, dv, dsk, dsv):
        ref[...] = jnp.zeros(ref.shape, ref.dtype)
    nothing = jnp.zeros((2, QBLK, DH), BF16)
    for there in range(1, chips):
        @pl.when(there > chip)
        def _():
            for half in range(2):
                skv[:, pl.ds((half * chips + there) * QBLK, QBLK), :] = nothing

    @pl.when(core == 0)
    def _():
        skv[:, aligned((chips + chip) * QBLK, QBLK), :] = nothing

    skv[:, aligned((core * chips + chip) * QBLK, QBLK), :] = kv[:, pl.ds(HALO, QBLK), :]

    @pl.when(blk == 0)
    def _():
        kv[:, pl.ds(0, HALO), :] = jnp.zeros((2, HALO, DH), BF16)

    for source in range(heads - 1, -1, -1):
        for which in range(2):
            arrive(which, source)
        if source == heads - 2:
            @pl.when(blk + 1 < blks)
            def _():
                halo(blk + 1).start()

    drain_keys()
    for step in range(1, heads):
        for which in range(2, 4):
            into(which, head, other(step)).start()

    for there in range(chips - 1):
        @pl.when(there < chip)
        def _():
            summary(there, chip).wait_recv()
            passed(core, there).start()

    for there in range(chips - 1):
        @pl.when(there < chip)
        def _():
            passed(1 - core, there).wait_recv()

    @pl.when(core == 1)
    def _():
        direct().wait_recv()

    for which in range(2, 4):
        own(which).wait()

    outs = ((dq, oq, 0), (bk, ok, HALO), (bv, ov, HALO))
    sets = ((dk, dsk, bk, FACTOR), (dv, dsv, bv, 1.0))

    def back(which, source, there):
        src, dst, skip = outs[which]
        return remote(
            src.at[aligned(skip + there * part, part)],
            dst.at[:, aligned(source * DH, DH)],
            send_out.at[which, there],
            recv_out.at[which, source],
            head=there,
        )

    def back_second(which, source):
        src, dst, skip = outs[which]
        return remote(
            src.at[pl.ds(skip + QBLK, rest)],
            dst.at[pl.ds(QBLK, rest), aligned(source * DH, DH)],
            send_out.at[which, 0],
            recv_out.at[which, source],
            head=0,
        )

    def back_first(which, source):
        src, dst, skip = outs[which]
        return remote(
            src.at[pl.ds(skip, QBLK)],
            dst.at[pl.ds(0, QBLK), aligned(source * DH, DH)],
            send_late.at[which],
            recv_late.at[which, source],
            head=0,
        )

    def keep(which):
        src, dst, skip = outs[which]
        return pltpu.make_async_copy(
            src.at[aligned(skip + head * part, part)], dst.at[:, aligned(head * DH, DH)], keep_out.at[which]
        )

    def keep_second(which):
        src, dst, skip = outs[which]
        return pltpu.make_async_copy(
            src.at[pl.ds(skip + QBLK, rest)], dst.at[pl.ds(QBLK, rest), pl.ds(0, DH)], keep_out.at[which]
        )

    def keep_first(which):
        src, dst, skip = outs[which]
        return pltpu.make_async_copy(
            src.at[pl.ds(skip, QBLK)], dst.at[pl.ds(0, QBLK), pl.ds(0, DH)], keep_late.at[which]
        )

    def send(which, there):
        @pl.when(head != there)
        def _():
            back(which, head, there).start()

        @pl.when(head == there)
        def _():
            keep(which).start()

    def handed():
        return remote(hand.at[0], hand.at[1], send_hand, recv_hand, blk=sibling)

    def partial(owner, source):
        return remote(
            sums.at[0, :, aligned(owner * QBLK, QBLK)],
            sums.at[1, :, aligned(source * QBLK, QBLK)],
            send_part.at[owner],
            recv_part.at[source],
            blk=owner * 2 + core,
        )

    def edge(there):
        return remote(edges.at[0], edges.at[1], send_edge, recv_edge, blk=there)

    def finish(there):
        at = aligned(HALO + there * part, part)
        for which in range(2):
            acc, _, out, scale = sets[which]
            out[at, :] = (acc[at, :] * scale).astype(BF16)
            send(1 + which, there)

    def finish_second():
        at = pl.ds(HALO + QBLK, rest)
        for which in range(2):
            acc, _, out, scale = sets[which]
            out[at, :] = (acc[at, :] * scale).astype(BF16)

            @pl.when(head > 0)
            def _():
                back_second(1 + which, head).start()

            @pl.when(head == 0)
            def _():
                keep_second(1 + which).start()

    def send_edges():
        @pl.when(blk > 0)
        def _():
            for which in range(2):
                acc, _, _, scale = sets[which]
                edges[0, which] = (acc[pl.ds(0, HALO), :] * scale).astype(BF16)
            edge(blk - 1).start()

    def finish_last():
        @pl.when(blk + 1 < blks)
        def _():
            edge(blk).wait_recv()
            for which in range(2):
                acc, _, _, scale = sets[which]
                acc[pl.ds(rows, HALO), :] += edges[1, which].astype(F32) * (1.0 / scale)

        for there in range(heads - 2, heads):
            finish(there)

    edges_at = jnp.maximum(place(0), place(1))
    last_at = jnp.maximum(edges_at + 2, jnp.maximum(place(heads - 2), place(heads - 1)))

    halo_at = jnp.minimum(place(0), place(1))

    def halo_for(step):
        @pl.when((blk > 0) & (step == halo_at))
        def _():
            halo(blk).wait_recv()

    half = chips * QBLK

    def hand_over(step):
        @pl.when(step == heads - 1)
        def _():
            for which in range(2):
                _, acc_sum, _, scale = sets[which]
                hand[0, which] = (acc_sum[aligned((1 - core) * half, half), :] * scale).astype(BF16)
            handed().start()

    def finish_at(step):
        for back_by in range(3):
            ready = chunk_at(step) - back_by

            @pl.when((ready > 0) & (ready < heads - 2) & (done_at(ready) == step))
            def _():
                finish(ready)

        @pl.when(done_at(0) == step)
        def _():
            finish_second()

    def step_of(step, carry):
        c = chunk_at(step)

        @pl.when(step > 0)
        def _():
            for which in range(2, 4):
                into(which, c, head).wait_recv()

        for pairs in range(1, chips // 2 + 1):
            @pl.when(chip // 2 + 1 == pairs)
            def _():
                attend(c, pairs, lambda: halo_for(step), lambda: hand_over(step), lq, lk, lv, lg, sk, sv, dq, dk, dv, dsk, dsv, live, scores, gprob)

        send(0, c)

        @pl.when(step < heads - 1)
        def _():
            finish_at(step)

        @pl.when(edges_at == step)
        def _():
            send_edges()

        @pl.when((last_at == step) & (step < heads - 1))
        def _():
            finish_last()

        return carry

    lax.fori_loop(0, heads, step_of, 0)

    handed().wait_recv()
    for which in range(2):
        acc, acc_sum, _, scale = sets[which]
        for there in range(chips - 1):
            @pl.when(there < chip)
            def _():
                at = pl.ds(there * QBLK, QBLK)
                mine = acc_sum[aligned(core * half + there * QBLK, QBLK), :] * scale
                sums[0, which, at, :] = (mine + hand[1, which, at, :].astype(F32)).astype(BF16)

    for there in range(chips - 1):
        @pl.when(there < chip)
        def _():
            partial(there, chip).start()

    finish_at(heads - 1)

    @pl.when(last_at >= heads - 1)
    def _():
        finish_last()

    for which in range(2):
        acc, acc_sum, _, scale = sets[which]
        at = aligned(chip * QBLK, QBLK)
        mine = acc[pl.ds(HALO, QBLK), :] + acc_sum[aligned(core * half + chip * QBLK, QBLK), :]
        block_sum[which] = mine * scale + hand[1, which, at, :].astype(F32)
    for source in range(chips - 1, 0, -1):
        @pl.when(source > chip)
        def _():
            partial(chip, source).wait_recv()
            block_sum[...] += sums[1, :, pl.ds(source * QBLK, QBLK), :].astype(F32)

    for which in range(2):
        out = sets[which][2]
        out[pl.ds(HALO, QBLK), :] = block_sum[which].astype(BF16)

        @pl.when(head > 0)
        def _():
            back_first(1 + which, head).start()

        @pl.when(head == 0)
        def _():
            keep_first(1 + which).start()

    drain_queries()
    drain_summary()
    handed().wait_send()
    for there in range(chips - 1):
        @pl.when(there < chip)
        def _():
            partial(there, chip).wait_send()

    @pl.when(blk > 0)
    def _():
        edge(blk - 1).wait_send()

    keep(0).wait()
    for step in range(1, heads):
        back(0, head, other(step)).wait_send()
        back(0, other(step), head).wait_recv()

    @pl.when(head == 0)
    def _():
        for which in range(1, 3):
            keep_second(which).wait()
            keep_first(which).wait()
            for there in range(1, heads):
                back(which, 0, there).wait_send()
                back_second(which, there).wait_recv()
                back_first(which, there).wait_recv()

    @pl.when(head > 0)
    def _():
        for which in range(1, 3):
            keep(which).wait()
            back_second(which, head).wait_send()
            back_first(which, head).wait_send()
            for there in range(1, heads):
                @pl.when(there != head)
                def _():
                    back(which, head, there).wait_send()
            for step in range(1, heads):
                back(which, other(step), head).wait_recv()


def copy_kernel(x, y, z, ox, oy, oz, held, read, written):
    pieces = read.shape[1]
    size = x.shape[0] // pieces

    def moves(which, piece):
        src, dst = ((x, ox), (y, oy), (z, oz))[which]
        at = pl.ds(piece * size, size)
        return (
            pltpu.make_async_copy(src.at[at], held.at[which, at], read.at[which, piece]),
            pltpu.make_async_copy(held.at[which, at], dst.at[at], written.at[which, piece]),
        )

    todo = [moves(which, piece) for piece in range(pieces) for which in range(3)]
    for first, _ in todo:
        first.start()
    for first, second in todo:
        first.wait()
        second.start()
    for _, second in todo:
        second.wait()


def body_of(heads, blks):
    def body(queries, key_in, values, grad_out, block_list):
        part, width = queries.shape
        rows, keys = heads * part, blks * QBLK
        dma = pltpu.SemaphoreType.DMA
        whole = pl.BlockSpec(memory_space=VMEM)
        far = pl.BlockSpec(memory_space=pltpu.HBM)
        result = (jax.ShapeDtypeStruct((part, width), BF16),) * 3
        found = pl.pallas_call(
            lambda *refs: fused(heads, blks, *refs),
            out_shape=result,
            in_specs=[whole] + [far] * 4,
            out_specs=[far] * 3,
            scratch_shapes=[
                VMEM((rows, DH), BF16),
                VMEM((rows, DH), BF16),
                VMEM((2, HALO + rows, DH), BF16),
                VMEM((2, keys, DH), BF16),
                VMEM((rows, DH), BF16),
                VMEM((HALO + rows, DH), F32),
                VMEM((HALO + rows, DH), F32),
                VMEM((keys, DH), F32),
                VMEM((keys, DH), F32),
                VMEM((HALO + rows, DH), BF16),
                VMEM((HALO + rows, DH), BF16),
                VMEM((2, 2, keys // 2, DH), BF16),
                VMEM((2, 2, keys // 2, DH), BF16),
                VMEM((2, 2, HALO, DH), BF16),
                VMEM((2, QBLK, DH), F32),
                VMEM((rows // CHUNK, SEGB, CHUNK), F32),
                VMEM((keys + WIDE, CHUNK), F32),
                VMEM((keys + WIDE, CHUNK), F32),
                dma((4, heads)),
                dma((4, heads)),
                dma((2, heads)),
                dma((2,)),
                dma((4,)),
                dma((blks // 2,)),
                dma((blks // 2,)),
                dma((blks // 2 + 1,)),
                dma((blks // 2 + 1,)),
                dma,
                dma,
                dma((3, heads)),
                dma((3, heads)),
                dma((3,)),
                dma((3,)),
                dma((3, heads)),
                dma((3,)),
                dma,
                dma,
                dma((blks // 2,)),
                dma((blks // 2,)),
                dma,
                dma,
            ],
            compiler_params=pltpu.CompilerParams(
                collective_id=0, has_side_effects=True, vmem_limit_bytes=62 * 1024 * 1024
            ),
            name="attention_backward",
        )(block_list.T, queries, key_in, values, grad_out)
        return pl.pallas_call(
            copy_kernel,
            out_shape=result,
            in_specs=[far] * 3,
            out_specs=[far] * 3,
            scratch_shapes=[VMEM((3, part, width), BF16), dma((3, 2)), dma((3, 2))],
            compiler_params=pltpu.CompilerParams(vmem_limit_bytes=62 * 1024 * 1024),
            name="results",
        )(*found)

    return body


def solution(mesh):
    placed = P(("blk", "head"), None)
    return jax.shard_map(
        body_of(mesh.shape["head"], mesh.shape["blk"]),
        mesh=mesh,
        in_specs=(placed,) * 4 + (P(),),
        out_specs=(placed,) * 3,
        check_vma=False,
    )
```

```python
import functools
import math

import jax
import jax.numpy as jnp
from jax import lax
from jax.experimental import pallas as pl
from jax.experimental.pallas import tpu as pltpu
from jax.sharding import PartitionSpec as P

DH = 128
QBLK = 128
MAXB = 16
SEGB = 16
HALO = 3 * QBLK
CHUNK = 2 * QBLK
WIDE = HALO + CHUNK
MESH = pl.DeviceIdType.MESH
VMEM = pltpu.VMEM
BF16 = jnp.bfloat16
F32 = jnp.float32
DEAD = -3e38
FACTOR = 1.0 / math.sqrt(DH)
NT = (((1,), (1,)), ((), ()))
TN = (((0,), (0,)), ((), ()))


def aligned(start, size):
    return pl.ds(pl.multiple_of(start, QBLK), size)


def remote(src, dst, send, recv, **where):
    return pltpu.make_async_remote_copy(
        src_ref=src,
        dst_ref=dst,
        send_sem=send,
        recv_sem=recv,
        device_id=where,
        device_id_type=MESH,
    )


def greet(heads, blks):
    head, blk = lax.axis_index("head"), lax.axis_index("blk")
    core = lax.rem(blk, 2)
    barrier = pltpu.get_barrier_semaphore()

    def signal(**where):
        pl.semaphore_signal(barrier, inc=1, device_id=where, device_id_type=MESH)

    for step in range(1, heads):
        signal(head=lax.rem(head + step, heads))
    for step in range(2, blks, 2):
        signal(blk=lax.rem(blk + step, blks))
    signal(blk=blk + 1 - 2 * core)
    near = blk - 1 + 2 * core
    has_near = (near >= 0) & (near < blks)

    @pl.when(has_near)
    def _():
        signal(blk=near)

    pl.semaphore_wait(barrier, heads - 1 + blks // 2 + has_near.astype(jnp.int32))


def mark_live(lists, live):
    blk = lax.axis_index("blk")
    blocks = lists.shape[1]
    chips = SEGB // 2

    def owner_of(shape):
        slot = lax.broadcasted_iota(jnp.int32, shape, 0)
        return 2 * lax.rem(slot, chips) + slot // chips

    owner = owner_of((SEGB, blocks))
    seen = jnp.zeros((SEGB, blocks), F32)
    for entry in range(MAXB):
        seen = jnp.where(lists[entry : entry + 1, :] == owner * SEGB, 1.0, seen)
    column = lax.broadcasted_iota(jnp.int32, (blocks, CHUNK), 0)
    query = lax.broadcasted_iota(jnp.int32, (blocks, CHUNK), 1) // QBLK
    slot = owner_of((SEGB, CHUNK)) * SEGB
    reader = lax.broadcasted_iota(jnp.int32, (SEGB, CHUNK), 1) // QBLK
    for c in range(live.shape[0]):
        first = blk * SEGB + 2 * c
        spread = jnp.where(column == query + first, 1.0, 0.0).astype(BF16)
        chosen = jnp.dot(seen.astype(BF16), spread, preferred_element_type=F32)
        live[c] = jnp.where(slot < reader + (first - 3), chosen, 0.0)


def attend(c, pairs, ready, q, k, v, g, sk, sv, dq, dk, dv, dsk, dsv, live, scores, gprob):
    blk = lax.axis_index("blk")
    keys = sk.shape[0]
    exp2_factor = FACTOR * math.log2(math.e)
    starts = [half + s * CHUNK for half in (0, keys // 2) for s in range(pairs)]
    base = pl.multiple_of(c * CHUNK, CHUNK)
    here = pl.ds(base, CHUNK)
    window = pl.ds(base, WIDE)
    queries, grads = q[here, :], g[here, :]
    slabs = [(pl.ds(s, CHUNK), pl.ds(s, CHUNK), sk, sv, dsk, dsv) for s in starts]
    slabs.append((pl.ds(keys, WIDE), window, k, v, dk, dv))

    tops, totals, dots = [], [], []
    for (at, rows, keys_of, values_of, _, _), start in zip(slabs, starts + [None]):
        if start is None:
            ready()
        raw = lax.dot_general(keys_of[rows, :], queries, NT, preferred_element_type=F32) * exp2_factor
        gp = lax.dot_general(values_of[rows, :], grads, NT, preferred_element_type=F32)
        if start is None:
            key_row = lax.broadcasted_iota(jnp.int32, (WIDE, CHUNK), 0)
            query_row = lax.broadcasted_iota(jnp.int32, (WIDE, CHUNK), 1)
            alive = (
                (key_row <= query_row + HALO)
                & ((key_row >= QBLK) | (query_row < QBLK))
                & ((blk > 0) | (key_row + base >= HALO))
            )
            masked = jnp.where(alive, raw, DEAD)
        else:
            masked = jnp.concatenate(
                [
                    jnp.where(live[c, pl.ds((start + sub) // QBLK, 1), :] > 0.5, raw[sub : sub + QBLK], DEAD)
                    for sub in range(0, CHUNK, QBLK)
                ],
                axis=0,
            )
        top = jnp.max(masked, axis=0, keepdims=True)
        weight = jnp.exp2(masked - top)
        scores[at, :] = weight
        gprob[at, :] = gp
        tops.append(top)
        totals.append(jnp.sum(weight, axis=0, keepdims=True))
        dots.append(jnp.sum(weight * gp, axis=0, keepdims=True))

    top = functools.reduce(jnp.maximum, tops)
    shares = [jnp.exp2(t - top) for t in tops]
    total = sum(t * share for t, share in zip(totals, shares))
    inverse = 1.0 / total
    row_dot = sum(t * share for t, share in zip(dots, shares)) * inverse

    query_grad = jnp.zeros((CHUNK, DH), F32)
    for (at, rows, keys_of, _, dk_of, dv_of), share in zip(slabs, shares):
        prob = scores[at, :] * (share * inverse)
        ds = (prob * (gprob[at, :] - row_dot)).astype(BF16)
        dv_of[rows, :] += jnp.dot(prob.astype(BF16), grads, preferred_element_type=F32)
        dk_of[rows, :] += jnp.dot(ds, queries, preferred_element_type=F32)
        query_grad += lax.dot_general(ds, keys_of[rows, :], TN, preferred_element_type=F32)
    dq[here, :] = (query_grad * FACTOR).astype(BF16)


def fused(
    heads, blks, lists, q, k, v, g, oq, ok, ov,
    lq, lg, kv, skv, dq, dk, dv, dsk, dsv, bk, bv, hand, sums, edges, block_sum, live, scores, gprob,
    send_in, recv_in, send_first, recv_first, send_own, send_sum, recv_sum, send_pass, recv_pass, send_halo,
    recv_halo, send_out, recv_out, keep_out, send_late, recv_late, keep_late, send_hand, recv_hand, send_part,
    recv_part, send_edge, recv_edge,
):
    head, blk = lax.axis_index("head"), lax.axis_index("blk")
    part = q.shape[0]
    rows = heads * part
    keys = blks * QBLK
    rest = part - QBLK
    chips = blks // 2
    chip, core = blk // 2, lax.rem(blk, 2)
    sibling = blk + 1 - 2 * core
    lk, lv = kv.at[0], kv.at[1]
    sk, sv = skv.at[0], skv.at[1]

    arrays = ((k, lk, HALO), (v, lv, HALO), (q, lq, 0), (g, lg, 0))

    def into(which, source, there):
        src, dst, skip = arrays[which]
        return remote(
            src.at[:, aligned(there * DH, DH)],
            dst.at[aligned(skip + source * part, part)],
            send_in.at[which, there],
            recv_in.at[which, source],
            head=there,
        )

    def first(which, there):
        src, dst, _ = arrays[which]
        return remote(
            src.at[pl.ds(0, QBLK), aligned(there * DH, DH)],
            dst.at[pl.ds(HALO, QBLK)],
            send_first.at[which, there],
            recv_first.at[which],
            head=there,
        )

    def second(which, there):
        src, dst, _ = arrays[which]
        return remote(
            src.at[pl.ds(QBLK, rest), aligned(there * DH, DH)],
            dst.at[pl.ds(HALO + QBLK, rest)],
            send_in.at[which, there],
            recv_in.at[which, 0],
            head=there,
        )

    def own(which):
        src, dst, skip = arrays[which]
        return pltpu.make_async_copy(
            src.at[:, aligned(head * DH, DH)], dst.at[aligned(skip + head * part, part)], send_own.at[which]
        )

    def other(step):
        return lax.rem(head + step, heads)

    def chunk_at(step):
        return lax.rem(head - step + heads, heads)

    place = chunk_at

    def done_at(c):
        late = jnp.maximum(place(c), place(jnp.minimum(c + 1, heads - 1)))
        return jnp.maximum(late, place(jnp.minimum(c + 2, heads - 1)))

    def slot(place_of, of_chip):
        return skv.at[:, aligned((place_of * chips + of_chip) * QBLK, QBLK)]

    def summary(of_chip, there):
        return remote(
            kv.at[:, pl.ds(HALO, QBLK)],
            slot(core, of_chip),
            send_sum.at[there],
            recv_sum.at[of_chip],
            blk=there * 2 + core,
        )

    def direct():
        return remote(
            kv.at[:, pl.ds(HALO, QBLK)], slot(0, chip), send_pass.at[chips], recv_pass.at[chips], blk=sibling
        )

    def passed(place_of, of_chip):
        return remote(
            slot(place_of, of_chip), slot(place_of, of_chip), send_pass.at[of_chip], recv_pass.at[of_chip], blk=sibling
        )

    def halo(there):
        return remote(kv.at[:, pl.ds(rows, HALO)], kv.at[:, pl.ds(0, HALO)], send_halo, recv_halo, blk=there)

    def arrive(which, source):
        @pl.when(head != source)
        def _():
            if which < 2 and isinstance(source, int) and source == 0:
                second(which, head).wait_recv()
            else:
                into(which, source, head).wait_recv()

    def drain_keys():
        @pl.when(head == 0)
        def _():
            for step in range(1, heads):
                for which in range(2):
                    first(which, step).wait_send()
                    second(which, step).wait_send()

        @pl.when(head > 0)
        def _():
            for step in range(1, heads):
                for which in range(2):
                    into(which, head, other(step)).wait_send()

    def drain_queries():
        for step in range(1, heads):
            for which in range(2, 4):
                into(which, head, other(step)).wait_send()

    def drain_summary():
        for there in range(1, chips):
            @pl.when(there > chip)
            def _():
                summary(chip, there).wait_send()

        @pl.when(core == 0)
        def _():
            direct().wait_send()

        for there in range(chips - 1):
            @pl.when(there < chip)
            def _():
                passed(core, there).wait_send()

        @pl.when(blk + 1 < blks)
        def _():
            halo(blk + 1).wait_send()

    greet(heads, blks)

    for which in range(4):
        own(which).start()

    @pl.when(head == 0)
    def _():
        for which in range(2):
            for step in range(1, heads):
                first(which, step).start()

    def send_keys(which):
        @pl.when(head == 0)
        def _():
            for step in range(1, heads):
                second(which, step).start()

        @pl.when(head > 0)
        def _():
            for step in range(1, heads):
                into(which, head, other(step)).start()

    send_keys(0)
    mark_live(lists, live)

    for which in range(2):
        own(which).wait()

        @pl.when(head > 0)
        def _():
            first(which, head).wait_recv()

    @pl.when(core == 0)
    def _():
        direct().start()

    for there in range(1, chips):
        @pl.when(there > chip)
        def _():
            summary(chip, there).start()

    send_keys(1)

    for ref in (dk, dv, dsk, dsv):
        ref[...] = jnp.zeros(ref.shape, ref.dtype)
    nothing = jnp.zeros((2, QBLK, DH), BF16)
    for there in range(1, chips):
        @pl.when(there > chip)
        def _():
            for half in range(2):
                skv[:, pl.ds((half * chips + there) * QBLK, QBLK), :] = nothing

    @pl.when(core == 0)
    def _():
        skv[:, aligned((chips + chip) * QBLK, QBLK), :] = nothing

    skv[:, aligned((core * chips + chip) * QBLK, QBLK), :] = kv[:, pl.ds(HALO, QBLK), :]

    @pl.when(blk == 0)
    def _():
        kv[:, pl.ds(0, HALO), :] = jnp.zeros((2, HALO, DH), BF16)

    for source in range(heads - 1, -1, -1):
        for which in range(2):
            arrive(which, source)
        if source == heads - 2:
            @pl.when(blk + 1 < blks)
            def _():
                halo(blk + 1).start()

    drain_keys()
    for which in range(2, 4):
        for step in range(1, heads):
            into(which, head, other(step)).start()

    for there in range(chips - 1):
        @pl.when(there < chip)
        def _():
            summary(there, chip).wait_recv()
            passed(core, there).start()

    for there in range(chips - 1):
        @pl.when(there < chip)
        def _():
            passed(1 - core, there).wait_recv()

    @pl.when(core == 1)
    def _():
        direct().wait_recv()

    for which in range(2, 4):
        own(which).wait()

    outs = ((dq, oq, 0), (bk, ok, HALO), (bv, ov, HALO))
    sets = ((dk, dsk, bk, FACTOR), (dv, dsv, bv, 1.0))

    def back(which, source, there):
        src, dst, skip = outs[which]
        return remote(
            src.at[aligned(skip + there * part, part)],
            dst.at[:, aligned(source * DH, DH)],
            send_out.at[which, there],
            recv_out.at[which, source],
            head=there,
        )

    def back_second(which, source):
        src, dst, skip = outs[which]
        return remote(
            src.at[pl.ds(skip + QBLK, rest)],
            dst.at[pl.ds(QBLK, rest), aligned(source * DH, DH)],
            send_out.at[which, 0],
            recv_out.at[which, source],
            head=0,
        )

    def back_first(which, source):
        src, dst, skip = outs[which]
        return remote(
            src.at[pl.ds(skip, QBLK)],
            dst.at[pl.ds(0, QBLK), aligned(source * DH, DH)],
            send_late.at[which],
            recv_late.at[which, source],
            head=0,
        )

    def keep(which):
        src, dst, skip = outs[which]
        return pltpu.make_async_copy(
            src.at[aligned(skip + head * part, part)], dst.at[:, aligned(head * DH, DH)], keep_out.at[which]
        )

    def keep_second(which):
        src, dst, skip = outs[which]
        return pltpu.make_async_copy(
            src.at[pl.ds(skip + QBLK, rest)], dst.at[pl.ds(QBLK, rest), pl.ds(0, DH)], keep_out.at[which]
        )

    def keep_first(which):
        src, dst, skip = outs[which]
        return pltpu.make_async_copy(
            src.at[pl.ds(skip, QBLK)], dst.at[pl.ds(0, QBLK), pl.ds(0, DH)], keep_late.at[which]
        )

    def send(which, there):
        @pl.when(head != there)
        def _():
            back(which, head, there).start()

        @pl.when(head == there)
        def _():
            keep(which).start()

    def handed():
        return remote(hand.at[0], hand.at[1], send_hand, recv_hand, blk=sibling)

    def partial(owner, source):
        return remote(
            sums.at[0, :, aligned(owner * QBLK, QBLK)],
            sums.at[1, :, aligned(source * QBLK, QBLK)],
            send_part.at[owner],
            recv_part.at[source],
            blk=owner * 2 + core,
        )

    def edge(there):
        return remote(edges.at[0], edges.at[1], send_edge, recv_edge, blk=there)

    def finish(there):
        at = aligned(HALO + there * part, part)
        for which in range(2):
            acc, _, out, scale = sets[which]
            out[at, :] = (acc[at, :] * scale).astype(BF16)
            send(1 + which, there)

    def finish_second():
        at = pl.ds(HALO + QBLK, rest)
        for which in range(2):
            acc, _, out, scale = sets[which]
            out[at, :] = (acc[at, :] * scale).astype(BF16)

            @pl.when(head > 0)
            def _():
                back_second(1 + which, head).start()

            @pl.when(head == 0)
            def _():
                keep_second(1 + which).start()

    def send_edges():
        @pl.when(blk > 0)
        def _():
            for which in range(2):
                acc, _, _, scale = sets[which]
                edges[0, which] = (acc[pl.ds(0, HALO), :] * scale).astype(BF16)
            edge(blk - 1).start()

    def finish_last():
        @pl.when(blk + 1 < blks)
        def _():
            edge(blk).wait_recv()
            for which in range(2):
                acc, _, _, scale = sets[which]
                acc[pl.ds(rows, HALO), :] += edges[1, which].astype(F32) * (1.0 / scale)

        for there in range(heads - 2, heads):
            finish(there)

    edges_at = jnp.maximum(place(0), place(1))
    last_at = jnp.maximum(edges_at + 2, jnp.maximum(place(heads - 2), place(heads - 1)))

    halo_at = jnp.minimum(place(0), place(1))

    def halo_for(step):
        @pl.when((blk > 0) & (step == halo_at))
        def _():
            halo(blk).wait_recv()

    half = chips * QBLK

    def finish_at(step):
        for back_by in range(3):
            ready = chunk_at(step) - back_by

            @pl.when((ready > 0) & (ready < heads - 2) & (done_at(ready) == step))
            def _():
                finish(ready)

        @pl.when(done_at(0) == step)
        def _():
            finish_second()

    def step_of(step, carry):
        c = chunk_at(step)

        @pl.when(step > 0)
        def _():
            for which in range(2, 4):
                into(which, c, head).wait_recv()

        for pairs in range(1, chips // 2 + 1):
            @pl.when(chip // 2 + 1 == pairs)
            def _():
                attend(c, pairs, lambda: halo_for(step), lq, lk, lv, lg, sk, sv, dq, dk, dv, dsk, dsv, live, scores, gprob)

        send(0, c)

        @pl.when(step < heads - 1)
        def _():
            finish_at(step)

        @pl.when(edges_at == step)
        def _():
            send_edges()

        @pl.when((last_at == step) & (step < heads - 1))
        def _():
            finish_last()

        return carry

    lax.fori_loop(0, heads, step_of, 0)

    for which in range(2):
        _, acc_sum, _, scale = sets[which]
        hand[0, which] = (acc_sum[aligned((1 - core) * half, half), :] * scale).astype(BF16)
    handed().start()
    handed().wait_recv()
    for which in range(2):
        acc, acc_sum, _, scale = sets[which]
        for there in range(chips - 1):
            @pl.when(there < chip)
            def _():
                at = pl.ds(there * QBLK, QBLK)
                mine = acc_sum[aligned(core * half + there * QBLK, QBLK), :] * scale
                sums[0, which, at, :] = (mine + hand[1, which, at, :].astype(F32)).astype(BF16)

    for there in range(chips - 1):
        @pl.when(there < chip)
        def _():
            partial(there, chip).start()

    finish_at(heads - 1)

    @pl.when(last_at >= heads - 1)
    def _():
        finish_last()

    for which in range(2):
        acc, acc_sum, _, scale = sets[which]
        at = aligned(chip * QBLK, QBLK)
        mine = acc[pl.ds(HALO, QBLK), :] + acc_sum[aligned(core * half + chip * QBLK, QBLK), :]
        block_sum[which] = mine * scale + hand[1, which, at, :].astype(F32)
    for source in range(chips - 1, 0, -1):
        @pl.when(source > chip)
        def _():
            partial(chip, source).wait_recv()
            block_sum[...] += sums[1, :, pl.ds(source * QBLK, QBLK), :].astype(F32)

    for which in range(2):
        out = sets[which][2]
        out[pl.ds(HALO, QBLK), :] = block_sum[which].astype(BF16)

        @pl.when(head > 0)
        def _():
            back_first(1 + which, head).start()

        @pl.when(head == 0)
        def _():
            keep_first(1 + which).start()

    drain_queries()
    drain_summary()
    handed().wait_send()
    for there in range(chips - 1):
        @pl.when(there < chip)
        def _():
            partial(there, chip).wait_send()

    @pl.when(blk > 0)
    def _():
        edge(blk - 1).wait_send()

    keep(0).wait()
    for step in range(1, heads):
        back(0, head, other(step)).wait_send()
        back(0, other(step), head).wait_recv()

    @pl.when(head == 0)
    def _():
        for which in range(1, 3):
            keep_second(which).wait()
            keep_first(which).wait()
            for there in range(1, heads):
                back(which, 0, there).wait_send()
                back_second(which, there).wait_recv()
                back_first(which, there).wait_recv()

    @pl.when(head > 0)
    def _():
        for which in range(1, 3):
            keep(which).wait()
            back_second(which, head).wait_send()
            back_first(which, head).wait_send()
            for there in range(1, heads):
                @pl.when(there != head)
                def _():
                    back(which, head, there).wait_send()
            for step in range(1, heads):
                back(which, other(step), head).wait_recv()


def copy_kernel(x, y, z, ox, oy, oz, held, read, written):
    pieces = read.shape[1]
    size = x.shape[0] // pieces

    def moves(which, piece):
        src, dst = ((x, ox), (y, oy), (z, oz))[which]
        at = pl.ds(piece * size, size)
        return (
            pltpu.make_async_copy(src.at[at], held.at[which, at], read.at[which, piece]),
            pltpu.make_async_copy(held.at[which, at], dst.at[at], written.at[which, piece]),
        )

    todo = [moves(which, piece) for piece in range(pieces) for which in range(3)]
    for first, _ in todo:
        first.start()
    for first, second in todo:
        first.wait()
        second.start()
    for _, second in todo:
        second.wait()


def body_of(heads, blks):
    def body(queries, key_in, values, grad_out, block_list):
        part, width = queries.shape
        rows, keys = heads * part, blks * QBLK
        dma = pltpu.SemaphoreType.DMA
        whole = pl.BlockSpec(memory_space=VMEM)
        far = pl.BlockSpec(memory_space=pltpu.HBM)
        result = (jax.ShapeDtypeStruct((part, width), BF16),) * 3
        found = pl.pallas_call(
            lambda *refs: fused(heads, blks, *refs),
            out_shape=result,
            in_specs=[whole] + [far] * 4,
            out_specs=[far] * 3,
            scratch_shapes=[
                VMEM((rows, DH), BF16),
                VMEM((rows, DH), BF16),
                VMEM((2, HALO + rows, DH), BF16),
                VMEM((2, keys, DH), BF16),
                VMEM((rows, DH), BF16),
                VMEM((HALO + rows, DH), F32),
                VMEM((HALO + rows, DH), F32),
                VMEM((keys, DH), F32),
                VMEM((keys, DH), F32),
                VMEM((HALO + rows, DH), BF16),
                VMEM((HALO + rows, DH), BF16),
                VMEM((2, 2, keys // 2, DH), BF16),
                VMEM((2, 2, keys // 2, DH), BF16),
                VMEM((2, 2, HALO, DH), BF16),
                VMEM((2, QBLK, DH), F32),
                VMEM((rows // CHUNK, SEGB, CHUNK), F32),
                VMEM((keys + WIDE, CHUNK), F32),
                VMEM((keys + WIDE, CHUNK), F32),
                dma((4, heads)),
                dma((4, heads)),
                dma((2, heads)),
                dma((2,)),
                dma((4,)),
                dma((blks // 2,)),
                dma((blks // 2,)),
                dma((blks // 2 + 1,)),
                dma((blks // 2 + 1,)),
                dma,
                dma,
                dma((3, heads)),
                dma((3, heads)),
                dma((3,)),
                dma((3,)),
                dma((3, heads)),
                dma((3,)),
                dma,
                dma,
                dma((blks // 2,)),
                dma((blks // 2,)),
                dma,
                dma,
            ],
            compiler_params=pltpu.CompilerParams(
                collective_id=0, has_side_effects=True, vmem_limit_bytes=62 * 1024 * 1024
            ),
            name="attention_backward",
        )(block_list.T, queries, key_in, values, grad_out)
        return pl.pallas_call(
            copy_kernel,
            out_shape=result,
            in_specs=[far] * 3,
            out_specs=[far] * 3,
            scratch_shapes=[VMEM((3, part, width), BF16), dma((3, 2)), dma((3, 2))],
            compiler_params=pltpu.CompilerParams(vmem_limit_bytes=62 * 1024 * 1024),
            name="results",
        )(*found)

    return body


def solution(mesh):
    placed = P(("blk", "head"), None)
    return jax.shard_map(
        body_of(mesh.shape["head"], mesh.shape["blk"]),
        mesh=mesh,
        in_specs=(placed,) * 4 + (P(),),
        out_specs=(placed,) * 3,
        check_vma=False,
    )
```

```python
import functools
import math

import jax
import jax.numpy as jnp
from jax import lax
from jax.experimental import pallas as pl
from jax.experimental.pallas import tpu as pltpu
from jax.sharding import PartitionSpec as P

DH = 128
QBLK = 128
MAXB = 16
SEGB = 16
HALO = 3 * QBLK
CHUNK = 2 * QBLK
WIDE = HALO + CHUNK
MESH = pl.DeviceIdType.MESH
VMEM = pltpu.VMEM
BF16 = jnp.bfloat16
F32 = jnp.float32
DEAD = -3e38
FACTOR = 1.0 / math.sqrt(DH)
NT = (((1,), (1,)), ((), ()))
TN = (((0,), (0,)), ((), ()))


def aligned(start, size):
    return pl.ds(pl.multiple_of(start, QBLK), size)


def remote(src, dst, send, recv, **where):
    return pltpu.make_async_remote_copy(
        src_ref=src,
        dst_ref=dst,
        send_sem=send,
        recv_sem=recv,
        device_id=where,
        device_id_type=MESH,
    )


def greet(heads, blks):
    head, blk = lax.axis_index("head"), lax.axis_index("blk")
    core = lax.rem(blk, 2)
    barrier = pltpu.get_barrier_semaphore()

    def signal(**where):
        pl.semaphore_signal(barrier, inc=1, device_id=where, device_id_type=MESH)

    for step in range(1, heads):
        signal(head=lax.rem(head + step, heads))
    for step in range(2, blks, 2):
        signal(blk=lax.rem(blk + step, blks))
    signal(blk=blk + 1 - 2 * core)
    near = blk - 1 + 2 * core
    has_near = (near >= 0) & (near < blks)

    @pl.when(has_near)
    def _():
        signal(blk=near)

    pl.semaphore_wait(barrier, heads - 1 + blks // 2 + has_near.astype(jnp.int32))


def mark_live(lists, live):
    blk = lax.axis_index("blk")
    blocks = lists.shape[1]
    chips = SEGB // 2

    def owner_of(shape):
        slot = lax.broadcasted_iota(jnp.int32, shape, 0)
        return 2 * lax.rem(slot, chips) + slot // chips

    owner = owner_of((SEGB, blocks))
    seen = jnp.zeros((SEGB, blocks), F32)
    for entry in range(MAXB):
        seen = jnp.where(lists[entry : entry + 1, :] == owner * SEGB, 1.0, seen)
    column = lax.broadcasted_iota(jnp.int32, (blocks, CHUNK), 0)
    query = lax.broadcasted_iota(jnp.int32, (blocks, CHUNK), 1) // QBLK
    slot = owner_of((SEGB, CHUNK)) * SEGB
    reader = lax.broadcasted_iota(jnp.int32, (SEGB, CHUNK), 1) // QBLK
    for c in range(live.shape[0]):
        first = blk * SEGB + 2 * c
        spread = jnp.where(column == query + first, 1.0, 0.0).astype(BF16)
        chosen = jnp.dot(seen.astype(BF16), spread, preferred_element_type=F32)
        live[c] = jnp.where(slot < reader + (first - 3), chosen, 0.0)


def attend(c, pairs, ready, q, k, v, g, sk, sv, dq, dk, dv, dsk, dsv, live, scores, gprob):
    blk = lax.axis_index("blk")
    keys = sk.shape[0]
    exp2_factor = FACTOR * math.log2(math.e)
    starts = [half + s * CHUNK for half in (0, keys // 2) for s in range(pairs)]
    base = pl.multiple_of(c * CHUNK, CHUNK)
    here = pl.ds(base, CHUNK)
    window = pl.ds(base, WIDE)
    queries, grads = q[here, :], g[here, :]
    slabs = [(pl.ds(s, CHUNK), pl.ds(s, CHUNK), sk, sv, dsk, dsv) for s in starts]
    slabs.append((pl.ds(keys, WIDE), window, k, v, dk, dv))

    tops, totals, dots = [], [], []
    for (at, rows, keys_of, values_of, _, _), start in zip(slabs, starts + [None]):
        if start is None:
            ready()
        raw = lax.dot_general(keys_of[rows, :], queries, NT, preferred_element_type=F32) * exp2_factor
        gp = lax.dot_general(values_of[rows, :], grads, NT, preferred_element_type=F32)
        if start is None:
            key_row = lax.broadcasted_iota(jnp.int32, (WIDE, CHUNK), 0)
            query_row = lax.broadcasted_iota(jnp.int32, (WIDE, CHUNK), 1)
            alive = (
                (key_row <= query_row + HALO)
                & ((key_row >= QBLK) | (query_row < QBLK))
                & ((blk > 0) | (key_row + base >= HALO))
            )
            masked = jnp.where(alive, raw, DEAD)
        else:
            masked = jnp.concatenate(
                [
                    jnp.where(live[c, pl.ds((start + sub) // QBLK, 1), :] > 0.5, raw[sub : sub + QBLK], DEAD)
                    for sub in range(0, CHUNK, QBLK)
                ],
                axis=0,
            )
        top = jnp.max(masked, axis=0, keepdims=True)
        weight = jnp.exp2(masked - top)
        scores[at, :] = weight
        gprob[at, :] = gp
        tops.append(top)
        totals.append(jnp.sum(weight, axis=0, keepdims=True))
        dots.append(jnp.sum(weight * gp, axis=0, keepdims=True))

    top = functools.reduce(jnp.maximum, tops)
    shares = [jnp.exp2(t - top) for t in tops]
    total = sum(t * share for t, share in zip(totals, shares))
    inverse = 1.0 / total
    row_dot = sum(t * share for t, share in zip(dots, shares)) * inverse

    query_grad = jnp.zeros((CHUNK, DH), F32)
    for (at, rows, keys_of, _, dk_of, dv_of), share in zip(slabs, shares):
        prob = scores[at, :] * (share * inverse)
        ds = (prob * (gprob[at, :] - row_dot)).astype(BF16)
        dv_of[rows, :] += jnp.dot(prob.astype(BF16), grads, preferred_element_type=F32)
        dk_of[rows, :] += jnp.dot(ds, queries, preferred_element_type=F32)
        query_grad += lax.dot_general(ds, keys_of[rows, :], TN, preferred_element_type=F32)
    dq[here, :] = (query_grad * FACTOR).astype(BF16)


def fused(
    heads, blks, lists, q, k, v, g, oq, ok, ov,
    lq, lg, kv, skv, dq, dk, dv, dsk, dsv, bk, bv, hand, sums, edges, block_sum, live, scores, gprob,
    send_in, recv_in, send_first, recv_first, send_own, send_sum, recv_sum, send_pass, recv_pass, send_halo,
    recv_halo, send_out, recv_out, keep_out, send_late, recv_late, keep_late, send_hand, recv_hand, send_part,
    recv_part, send_edge, recv_edge,
):
    head, blk = lax.axis_index("head"), lax.axis_index("blk")
    part = q.shape[0]
    rows = heads * part
    keys = blks * QBLK
    rest = part - QBLK
    chips = blks // 2
    chip, core = blk // 2, lax.rem(blk, 2)
    sibling = blk + 1 - 2 * core
    lk, lv = kv.at[0], kv.at[1]
    sk, sv = skv.at[0], skv.at[1]

    arrays = ((k, lk, HALO), (v, lv, HALO), (q, lq, 0), (g, lg, 0))

    def into(which, source, there):
        src, dst, skip = arrays[which]
        return remote(
            src.at[:, aligned(there * DH, DH)],
            dst.at[aligned(skip + source * part, part)],
            send_in.at[which, there],
            recv_in.at[which, source],
            head=there,
        )

    def first(which, there):
        src, dst, _ = arrays[which]
        return remote(
            src.at[pl.ds(0, QBLK), aligned(there * DH, DH)],
            dst.at[pl.ds(HALO, QBLK)],
            send_first.at[which, there],
            recv_first.at[which],
            head=there,
        )

    def second(which, there):
        src, dst, _ = arrays[which]
        return remote(
            src.at[pl.ds(QBLK, rest), aligned(there * DH, DH)],
            dst.at[pl.ds(HALO + QBLK, rest)],
            send_in.at[which, there],
            recv_in.at[which, 0],
            head=there,
        )

    def own(which):
        src, dst, skip = arrays[which]
        return pltpu.make_async_copy(
            src.at[:, aligned(head * DH, DH)], dst.at[aligned(skip + head * part, part)], send_own.at[which]
        )

    def other(step):
        return lax.rem(head + step, heads)

    def chunk_at(step):
        return lax.rem(head - step + heads, heads)

    place = chunk_at

    def done_at(c):
        late = jnp.maximum(place(c), place(jnp.minimum(c + 1, heads - 1)))
        return jnp.maximum(late, place(jnp.minimum(c + 2, heads - 1)))

    def slot(place_of, of_chip):
        return skv.at[:, aligned((place_of * chips + of_chip) * QBLK, QBLK)]

    def summary(of_chip, there):
        return remote(
            kv.at[:, pl.ds(HALO, QBLK)],
            slot(core, of_chip),
            send_sum.at[there],
            recv_sum.at[of_chip],
            blk=there * 2 + core,
        )

    def direct():
        return remote(
            kv.at[:, pl.ds(HALO, QBLK)], slot(0, chip), send_pass.at[chips], recv_pass.at[chips], blk=sibling
        )

    def passed(place_of, of_chip):
        return remote(
            slot(place_of, of_chip), slot(place_of, of_chip), send_pass.at[of_chip], recv_pass.at[of_chip], blk=sibling
        )

    def halo(there):
        return remote(kv.at[:, pl.ds(rows, HALO)], kv.at[:, pl.ds(0, HALO)], send_halo, recv_halo, blk=there)

    def arrive(which, source):
        @pl.when(head != source)
        def _():
            if which < 2 and isinstance(source, int) and source == 0:
                second(which, head).wait_recv()
            else:
                into(which, source, head).wait_recv()

    def drain_keys():
        @pl.when(head == 0)
        def _():
            for step in range(1, heads):
                for which in range(2):
                    first(which, step).wait_send()
                    second(which, step).wait_send()

        @pl.when(head > 0)
        def _():
            for step in range(1, heads):
                for which in range(2):
                    into(which, head, other(step)).wait_send()

    def drain_queries():
        for step in range(1, heads):
            for which in range(2, 4):
                into(which, head, other(step)).wait_send()

    def drain_summary():
        for there in range(1, chips):
            @pl.when(there > chip)
            def _():
                summary(chip, there).wait_send()

        @pl.when(core == 0)
        def _():
            direct().wait_send()

        for there in range(chips - 1):
            @pl.when(there < chip)
            def _():
                passed(core, there).wait_send()

        @pl.when(blk + 1 < blks)
        def _():
            halo(blk + 1).wait_send()

    greet(heads, blks)

    for which in range(4):
        own(which).start()

    @pl.when(head == 0)
    def _():
        for which in range(2):
            for step in range(1, heads):
                first(which, step).start()

    def send_keys(which):
        @pl.when(head == 0)
        def _():
            for step in range(1, heads):
                second(which, step).start()

        @pl.when(head > 0)
        def _():
            for step in range(1, heads):
                into(which, head, other(step)).start()

    send_keys(0)
    mark_live(lists, live)

    for which in range(2):
        own(which).wait()

        @pl.when(head > 0)
        def _():
            first(which, head).wait_recv()

    @pl.when(core == 0)
    def _():
        direct().start()

    for there in range(1, chips):
        @pl.when(there > chip)
        def _():
            summary(chip, there).start()

    send_keys(1)

    for ref in (dk, dv, dsk, dsv):
        ref[...] = jnp.zeros(ref.shape, ref.dtype)
    nothing = jnp.zeros((2, QBLK, DH), BF16)
    for there in range(1, chips):
        @pl.when(there > chip)
        def _():
            for half in range(2):
                skv[:, pl.ds((half * chips + there) * QBLK, QBLK), :] = nothing

    @pl.when(core == 0)
    def _():
        skv[:, aligned((chips + chip) * QBLK, QBLK), :] = nothing

    skv[:, aligned((core * chips + chip) * QBLK, QBLK), :] = kv[:, pl.ds(HALO, QBLK), :]

    @pl.when(blk == 0)
    def _():
        kv[:, pl.ds(0, HALO), :] = jnp.zeros((2, HALO, DH), BF16)

    for source in range(heads - 1, -1, -1):
        for which in range(2):
            arrive(which, source)
        if source == heads - 2:
            @pl.when(blk + 1 < blks)
            def _():
                halo(blk + 1).start()

    drain_keys()
    for which in range(2, 4):
        for step in range(1, heads):
            into(which, head, other(step)).start()

    for there in range(chips - 1):
        @pl.when(there < chip)
        def _():
            summary(there, chip).wait_recv()
            passed(core, there).start()

    for there in range(chips - 1):
        @pl.when(there < chip)
        def _():
            passed(1 - core, there).wait_recv()

    @pl.when(core == 1)
    def _():
        direct().wait_recv()

    for which in range(2, 4):
        own(which).wait()

    outs = ((dq, oq, 0), (bk, ok, HALO), (bv, ov, HALO))
    sets = ((dk, dsk, bk, FACTOR), (dv, dsv, bv, 1.0))

    def back(which, source, there):
        src, dst, skip = outs[which]
        return remote(
            src.at[aligned(skip + there * part, part)],
            dst.at[:, aligned(source * DH, DH)],
            send_out.at[which, there],
            recv_out.at[which, source],
            head=there,
        )

    def back_second(which, source):
        src, dst, skip = outs[which]
        return remote(
            src.at[pl.ds(skip + QBLK, rest)],
            dst.at[pl.ds(QBLK, rest), aligned(source * DH, DH)],
            send_out.at[which, 0],
            recv_out.at[which, source],
            head=0,
        )

    def back_first(which, source):
        src, dst, skip = outs[which]
        return remote(
            src.at[pl.ds(skip, QBLK)],
            dst.at[pl.ds(0, QBLK), aligned(source * DH, DH)],
            send_late.at[which],
            recv_late.at[which, source],
            head=0,
        )

    def keep(which):
        src, dst, skip = outs[which]
        return pltpu.make_async_copy(
            src.at[aligned(skip + head * part, part)], dst.at[:, aligned(head * DH, DH)], keep_out.at[which]
        )

    def keep_second(which):
        src, dst, skip = outs[which]
        return pltpu.make_async_copy(
            src.at[pl.ds(skip + QBLK, rest)], dst.at[pl.ds(QBLK, rest), pl.ds(0, DH)], keep_out.at[which]
        )

    def keep_first(which):
        src, dst, skip = outs[which]
        return pltpu.make_async_copy(
            src.at[pl.ds(skip, QBLK)], dst.at[pl.ds(0, QBLK), pl.ds(0, DH)], keep_late.at[which]
        )

    def send(which, there):
        @pl.when(head != there)
        def _():
            back(which, head, there).start()

        @pl.when(head == there)
        def _():
            keep(which).start()

    def handed():
        return remote(hand.at[0], hand.at[1], send_hand, recv_hand, blk=sibling)

    def partial(owner, source):
        return remote(
            sums.at[0, :, aligned(owner * QBLK, QBLK)],
            sums.at[1, :, aligned(source * QBLK, QBLK)],
            send_part.at[owner],
            recv_part.at[source],
            blk=owner * 2 + core,
        )

    def edge(there):
        return remote(edges.at[0], edges.at[1], send_edge, recv_edge, blk=there)

    def finish(there):
        at = aligned(HALO + there * part, part)
        for which in range(2):
            acc, _, out, scale = sets[which]
            out[at, :] = (acc[at, :] * scale).astype(BF16)
            send(1 + which, there)

    def finish_second():
        at = pl.ds(HALO + QBLK, rest)
        for which in range(2):
            acc, _, out, scale = sets[which]
            out[at, :] = (acc[at, :] * scale).astype(BF16)

            @pl.when(head > 0)
            def _():
                back_second(1 + which, head).start()

            @pl.when(head == 0)
            def _():
                keep_second(1 + which).start()

    def send_edges():
        @pl.when(blk > 0)
        def _():
            for which in range(2):
                acc, _, _, scale = sets[which]
                edges[0, which] = (acc[pl.ds(0, HALO), :] * scale).astype(BF16)
            edge(blk - 1).start()

    def finish_last():
        @pl.when(blk + 1 < blks)
        def _():
            edge(blk).wait_recv()
            for which in range(2):
                acc, _, _, scale = sets[which]
                acc[pl.ds(rows, HALO), :] += edges[1, which].astype(F32) * (1.0 / scale)

        for there in range(heads - 2, heads):
            finish(there)

    edges_at = jnp.maximum(place(0), place(1))
    last_at = jnp.maximum(edges_at + 2, jnp.maximum(place(heads - 2), place(heads - 1)))

    halo_at = jnp.minimum(place(0), place(1))

    def halo_for(step):
        @pl.when((blk > 0) & (step == halo_at))
        def _():
            halo(blk).wait_recv()

    half = chips * QBLK

    def finish_at(step):
        for back_by in range(3):
            ready = chunk_at(step) - back_by

            @pl.when((ready > 0) & (ready < heads - 2) & (done_at(ready) == step))
            def _():
                finish(ready)

        @pl.when(done_at(0) == step)
        def _():
            finish_second()

    def step_of(step, carry):
        c = chunk_at(step)

        @pl.when(step > 0)
        def _():
            for which in range(2, 4):
                into(which, c, head).wait_recv()

        for pairs in range(1, chips // 2 + 1):
            @pl.when(chip // 2 + 1 == pairs)
            def _():
                attend(c, pairs, lambda: halo_for(step), lq, lk, lv, lg, sk, sv, dq, dk, dv, dsk, dsv, live, scores, gprob)

        @pl.when(edges_at == step)
        def _():
            send_edges()

        send(0, c)

        @pl.when(step < heads - 1)
        def _():
            finish_at(step)

        @pl.when((last_at == step) & (step < heads - 1))
        def _():
            finish_last()

        return carry

    lax.fori_loop(0, heads, step_of, 0)

    for which in range(2):
        _, acc_sum, _, scale = sets[which]
        hand[0, which] = (acc_sum[aligned((1 - core) * half, half), :] * scale).astype(BF16)
    handed().start()
    handed().wait_recv()
    for which in range(2):
        acc, acc_sum, _, scale = sets[which]
        for there in range(chips - 1):
            @pl.when(there < chip)
            def _():
                at = pl.ds(there * QBLK, QBLK)
                mine = acc_sum[aligned(core * half + there * QBLK, QBLK), :] * scale
                sums[0, which, at, :] = (mine + hand[1, which, at, :].astype(F32)).astype(BF16)

    for there in range(chips - 1):
        @pl.when(there < chip)
        def _():
            partial(there, chip).start()

    finish_at(heads - 1)

    @pl.when(last_at >= heads - 1)
    def _():
        finish_last()

    for which in range(2):
        acc, acc_sum, _, scale = sets[which]
        at = aligned(chip * QBLK, QBLK)
        mine = acc[pl.ds(HALO, QBLK), :] + acc_sum[aligned(core * half + chip * QBLK, QBLK), :]
        block_sum[which] = mine * scale + hand[1, which, at, :].astype(F32)
    for source in range(chips - 1, 0, -1):
        @pl.when(source > chip)
        def _():
            partial(chip, source).wait_recv()
            block_sum[...] += sums[1, :, pl.ds(source * QBLK, QBLK), :].astype(F32)

    for which in range(2):
        out = sets[which][2]
        out[pl.ds(HALO, QBLK), :] = block_sum[which].astype(BF16)

        @pl.when(head > 0)
        def _():
            back_first(1 + which, head).start()

        @pl.when(head == 0)
        def _():
            keep_first(1 + which).start()

    drain_queries()
    drain_summary()
    handed().wait_send()
    for there in range(chips - 1):
        @pl.when(there < chip)
        def _():
            partial(there, chip).wait_send()

    @pl.when(blk > 0)
    def _():
        edge(blk - 1).wait_send()

    keep(0).wait()
    for step in range(1, heads):
        back(0, head, other(step)).wait_send()
        back(0, other(step), head).wait_recv()

    @pl.when(head == 0)
    def _():
        for which in range(1, 3):
            keep_second(which).wait()
            keep_first(which).wait()
            for there in range(1, heads):
                back(which, 0, there).wait_send()
                back_second(which, there).wait_recv()
                back_first(which, there).wait_recv()

    @pl.when(head > 0)
    def _():
        for which in range(1, 3):
            keep(which).wait()
            back_second(which, head).wait_send()
            back_first(which, head).wait_send()
            for there in range(1, heads):
                @pl.when(there != head)
                def _():
                    back(which, head, there).wait_send()
            for step in range(1, heads):
                back(which, other(step), head).wait_recv()


def copy_kernel(x, y, z, ox, oy, oz, held, read, written):
    pieces = read.shape[1]
    size = x.shape[0] // pieces

    def moves(which, piece):
        src, dst = ((x, ox), (y, oy), (z, oz))[which]
        at = pl.ds(piece * size, size)
        return (
            pltpu.make_async_copy(src.at[at], held.at[which, at], read.at[which, piece]),
            pltpu.make_async_copy(held.at[which, at], dst.at[at], written.at[which, piece]),
        )

    todo = [moves(which, piece) for piece in range(pieces) for which in range(3)]
    for first, _ in todo:
        first.start()
    for first, second in todo:
        first.wait()
        second.start()
    for _, second in todo:
        second.wait()


def body_of(heads, blks):
    def body(queries, key_in, values, grad_out, block_list):
        part, width = queries.shape
        rows, keys = heads * part, blks * QBLK
        dma = pltpu.SemaphoreType.DMA
        whole = pl.BlockSpec(memory_space=VMEM)
        far = pl.BlockSpec(memory_space=pltpu.HBM)
        result = (jax.ShapeDtypeStruct((part, width), BF16),) * 3
        found = pl.pallas_call(
            lambda *refs: fused(heads, blks, *refs),
            out_shape=result,
            in_specs=[whole] + [far] * 4,
            out_specs=[far] * 3,
            scratch_shapes=[
                VMEM((rows, DH), BF16),
                VMEM((rows, DH), BF16),
                VMEM((2, HALO + rows, DH), BF16),
                VMEM((2, keys, DH), BF16),
                VMEM((rows, DH), BF16),
                VMEM((HALO + rows, DH), F32),
                VMEM((HALO + rows, DH), F32),
                VMEM((keys, DH), F32),
                VMEM((keys, DH), F32),
                VMEM((HALO + rows, DH), BF16),
                VMEM((HALO + rows, DH), BF16),
                VMEM((2, 2, keys // 2, DH), BF16),
                VMEM((2, 2, keys // 2, DH), BF16),
                VMEM((2, 2, HALO, DH), BF16),
                VMEM((2, QBLK, DH), F32),
                VMEM((rows // CHUNK, SEGB, CHUNK), F32),
                VMEM((keys + WIDE, CHUNK), F32),
                VMEM((keys + WIDE, CHUNK), F32),
                dma((4, heads)),
                dma((4, heads)),
                dma((2, heads)),
                dma((2,)),
                dma((4,)),
                dma((blks // 2,)),
                dma((blks // 2,)),
                dma((blks // 2 + 1,)),
                dma((blks // 2 + 1,)),
                dma,
                dma,
                dma((3, heads)),
                dma((3, heads)),
                dma((3,)),
                dma((3,)),
                dma((3, heads)),
                dma((3,)),
                dma,
                dma,
                dma((blks // 2,)),
                dma((blks // 2,)),
                dma,
                dma,
            ],
            compiler_params=pltpu.CompilerParams(
                collective_id=0, has_side_effects=True, vmem_limit_bytes=62 * 1024 * 1024
            ),
            name="attention_backward",
        )(block_list.T, queries, key_in, values, grad_out)
        return pl.pallas_call(
            copy_kernel,
            out_shape=result,
            in_specs=[far] * 3,
            out_specs=[far] * 3,
            scratch_shapes=[VMEM((3, part, width), BF16), dma((3, 2)), dma((3, 2))],
            compiler_params=pltpu.CompilerParams(vmem_limit_bytes=62 * 1024 * 1024),
            name="results",
        )(*found)

    return body


def solution(mesh):
    placed = P(("blk", "head"), None)
    return jax.shard_map(
        body_of(mesh.shape["head"], mesh.shape["blk"]),
        mesh=mesh,
        in_specs=(placed,) * 4 + (P(),),
        out_specs=(placed,) * 3,
        check_vma=False,
    )
```
